128 devices in a mesh: tm: 16 (over x, y_hi, core), freq: 8 (over z, y_lo).
Axes of the slice: x: 4, y: 4 (y_hi: 2, y_lo: 2; y = y_hi * 2 + y_lo), z: 4, core: 2. Of those that a mesh axis runs over, the one named last changes fastest.
Arguments:
- visibilities: bfloat16 [2, 128, 768, 4096], P(None, None, 'freq', 'tm'), may hold values from -6 to 6
- counts: int32 [128], replicated, may hold values from 1 to 255
- beam_inverse: bfloat16 [64, 768, 2, 64, 128], P('tm', 'freq'), may hold values from -0.375 to 0.375
- kl_modes: bfloat16 [64, 128, 768], P('tm'), may hold values from -0.21875 to 0.21875
Outputs:
- filtered: bfloat16 [64, 64, 2, 128], P('freq', 'tm')
The draws below stay inside these ranges and needn't reach their ends.
All inputs are finite; a program needn't handle non-finite values.
Results may differ from the reference program's by a relative error of at most 0.0085.
Values may be sent and summed in bfloat16 or wider, within the bound.
A program may use at most 128 MiB of HBM per device.

```python
import math
import jax
import jax.numpy as jnp
from jax import lax

B = 128
F = 768
TIMES = 4096
L = 64
KK = 128
MW = 64
N_FREQ = 8


def draw_visibilities(key, part):
    key = jax.random.fold_in(key, 11)
    keys = jax.random.split(key, 5)
    lead = (2, B, F, 1)
    times = jnp.arange(TIMES, dtype=jnp.int32)
    near_modes = MW + jax.random.randint(keys[0], lead, 0, MW)
    far_modes = 2 * MW + jax.random.randint(keys[1], lead, 0, 3 * MW)
    near_phase = jax.random.uniform(keys[2], lead, jnp.float32, 0.0, 2.0 * math.pi)
    far_phase = jax.random.uniform(keys[3], lead, jnp.float32, 0.0, 2.0 * math.pi)
    white = 0.7 * jax.random.truncated_normal(keys[4], -3.0, 3.0, (2, B, F, TIMES), jnp.float32)
    near_amp = 1.8
    far_amp = 1.8
    near_angle = (near_modes * times % TIMES).astype(jnp.float32) * (2.0 * math.pi / TIMES) + near_phase
    far_angle = (far_modes * times % TIMES).astype(jnp.float32) * (2.0 * math.pi / TIMES) + far_phase
    values = white + near_amp * jnp.cos(near_angle) + far_amp * jnp.cos(far_angle)
    return values.astype(jnp.bfloat16)


def set_ends(drawn, rng, low, largest):
    longest = drawn.shape.index(max(drawn.shape))
    spots = []
    for shift in (0, 1):
        where = [jax.random.randint(jax.random.fold_in(rng, axis), (), 0, length) for axis, length in enumerate(drawn.shape)]
        where[longest] = (where[longest] + shift) % drawn.shape[longest]
        spots.append(tuple(where))
    return drawn.at[spots[0]].set(low).at[spots[1]].set(largest)


def levels(key, dims, cuts, smallest, top_value):
    def one(axis_at, shards_of):
        steps = jax.random.uniform(jax.random.fold_in(jax.random.fold_in(key, 6), axis_at), (shards_of,), jnp.float32, smallest / len(cuts), top_value / len(cuts))
        return jnp.repeat(jnp.exp(steps), dims[axis_at] // shards_of).reshape((-1,) + (1,) * (len(dims) - axis_at - 1))

    loudness = one(*cuts[0])
    for cut in cuts[1:]:
        loudness = loudness * one(*cut)
    return loudness


def noise(own_key, dims, width, reach, cuts=(), kind=jnp.bfloat16):
    values = width * jax.random.normal(own_key, dims, jnp.float32)
    if cuts:
        values = values * levels(own_key, dims, cuts, -0.22, 0.18)
    return jnp.clip(values, -reach, reach).astype(kind)


def setup_inputs(seed: int = 0) -> dict:
    arg_keys = jax.random.split(jax.random.key(seed), 5)
    visibilities = draw_visibilities(jax.random.fold_in(arg_keys[4], 71), 0)
    counts = set_ends(jax.random.randint(arg_keys[1], (B,), 1, 256), jax.random.fold_in(arg_keys[1], 1), 1, 255).astype(jnp.int32)
    beam_inverse = noise(arg_keys[2], (MW, F, 2, L, B), (2 * B) ** -0.5, 0.375, ((0, 16), (1, 8)))
    kl_modes = noise(arg_keys[3], (MW, KK, F), F ** -0.5, 0.21875, ((0, 16),))
    return {"visibilities": visibilities, "counts": counts, "beam_inverse": beam_inverse, "kl_modes": kl_modes}


def dft_table(modes, times, total):
    phase = modes[:, None] * times[None, :] % total
    angle = phase.astype(jnp.float32) * (2.0 * math.pi / total)
    cosine = jnp.cos(angle)
    sine = jnp.sin(angle)
    table = jnp.stack([jnp.stack([cosine, sine], 1), jnp.stack([-sine, cosine], 1)], 1)
    return table.astype(jnp.bfloat16)

def reference(visibilities, counts, beam_inverse, kl_modes):
    modes = jnp.arange(MW, dtype=jnp.int32)
    times = jnp.arange(TIMES, dtype=jnp.int32)
    table = dft_table(modes, times, TIMES).astype(jnp.float32)
    band = F // N_FREQ
    blocks = jnp.moveaxis(visibilities.reshape(2, B, N_FREQ, band, TIMES), 2, 0)

    def one_block(block):
        return jnp.einsum('mqpt,pbft->mqbf', table, block.astype(jnp.float32))
    pieces = lax.map(one_block, blocks)
    transform = jnp.moveaxis(pieces, 0, 3).reshape(MW, 2, B, F)
    factor = jnp.sqrt(counts.astype(jnp.float32)) * (1.0 / math.sqrt(128.0 * TIMES))
    spectrum = (transform * factor[None, None, :, None]).astype(jnp.bfloat16)

    def one_mode(pair):
        beam, spec = pair
        terms = jnp.einsum('fplb,qbf->pqlf', beam.astype(jnp.float32), spec.astype(jnp.float32))
        return jnp.stack([terms[0, 0] - terms[1, 1], terms[0, 1] + terms[1, 0]], 0).astype(jnp.bfloat16)
    sky = lax.map(one_mode, (beam_inverse, spectrum))
    filtered = jnp.einsum('mkf,mqlf->lmqk', kl_modes.astype(jnp.float32), sky.astype(jnp.float32))
    return filtered.astype(jnp.bfloat16)
```

```python
import functools
import math

import jax
import jax.numpy as jnp
import ml_dtypes
import numpy as np
from jax import lax
from jax.experimental import pallas as pl
from jax.experimental.pallas import tpu as pltpu
from jax.sharding import PartitionSpec as P

RANK = 12
STRONG = (2, 3, 4, 5)
ROWS = 2 * RANK + 2 * len(STRONG)
F32 = jnp.float32
BF16 = jnp.bfloat16


def window_factors(modes, window, windows):
    total = window * windows
    step = 2.0 * math.pi / total
    m = np.arange(modes, dtype=np.float64)
    t = np.arange(window, dtype=np.float64)
    mc, tc = (modes - 1) / 2.0, (window - 1) / 2.0
    diag = -np.cos(math.pi * (2 * t + 1 - window) / total) * math.cos(math.pi * modes / total)
    off = np.sin(math.pi * (t[:-1] + 1) / total) * np.sin(math.pi * (window - 1 - t[:-1]) / total)
    _, vectors = np.linalg.eigh(np.diag(diag) + np.diag(off, 1) + np.diag(off, -1))
    return m, t, mc, tc, step, vectors


def prolate(modes, window, windows):
    m, t, mc, tc, step, vectors = window_factors(modes, window, windows)
    centred = np.exp(-1j * step * np.outer(m - mc, t - tc))
    strength = np.linalg.norm(centred @ vectors, axis=0)
    basis = vectors[:, np.argsort(-strength)[:RANK]].T
    basis = basis * np.sign(basis[:, :window // 3].sum(1))[:, None]
    expand = centred @ basis.T
    project = basis * np.exp(-1j * step * mc * (t - tc))[None]
    return m, tc, step, expand, project


def halves(x):
    x = np.round(x * 2.0**22) / 2.0**22
    high = x.astype(np.float32).astype(ml_dtypes.bfloat16)
    low = (x - high.astype(np.float64)).astype(np.float32).astype(ml_dtypes.bfloat16)
    return np.concatenate([high, low], 0)


def factors(modes, window, windows):
    m, tc, step, expand, project = prolate(modes, window, windows)
    order = list(STRONG) + [k for k in range(RANK) if k not in STRONG]
    lead = len(STRONG)
    rows = [(k, part) for part in (0, 1) for k in order[:lead]]
    rows += [(k, part) for part in (0, 1) for k in order[lead:]]
    g = np.zeros((2 * RANK, 2, window))
    for at, (k, part) in enumerate(rows):
        re, im = project[k].real, project[k].imag
        g[at] = (re, -im) if part == 0 else (im, re)
    e = np.zeros((modes, 2, windows, ROWS))
    for w in range(windows):
        turned = expand * np.exp(-1j * step * m * (w * window + tc))[:, None]
        for at, (k, part) in enumerate(rows):
            re, im = turned[:, k].real, turned[:, k].imag
            e[:, 0, w, at] = re if part == 0 else -im
            e[:, 1, w, at] = im if part == 0 else re
    e[..., 2 * RANK:] = e[..., :2 * lead]
    return halves(g.reshape(2 * RANK, 2 * window)), halves(e.reshape(2 * modes, windows * ROWS))


def kernel(
    counts, vis, beam, kl, g, e, out,
    visb, beamb, klb, klp, gb, eb, ysend, yrecv, ssend, srecv, wf, wmat, skysend, skyrecv,
    vis_sem, beam_sem, misc_sem, ys_sem, yr_sem, ss_sem, sr_sem, ks_sem, kr_sem,
    *, tm, nf, total,
):
    me = lax.axis_index("tm")
    mf = lax.axis_index("freq")
    lanes = visb.shape[2]
    half = lanes // 2
    modes = beamb.shape[0]
    band = beamb.shape[1]
    window = visb.shape[3]

    g_copy = pltpu.make_async_copy(g, gb, misc_sem.at[0])
    e_copy = pltpu.make_async_copy(e, eb, misc_sem.at[1])
    kl_copy = pltpu.make_async_copy(kl, klb, misc_sem.at[2])
    g_copy.start()

    def vis_copy(j):
        return pltpu.make_async_copy(vis.at[:, j], visb.at[j], vis_sem.at[j])

    def beam_copy(m):
        return pltpu.make_async_copy(beam.at[m], beamb.at[m], beam_sem.at[m])

    def start_vis(d, c):
        vis_copy(lax.rem(me + d, tm)).start()
        return c

    lax.fori_loop(1, tm + 1, start_vis, 0)
    e_copy.start()
    kl_copy.start()
    for m in range(modes):
        beam_copy(m).start()

    barrier = pltpu.get_barrier_semaphore()

    def greet_tm(d, c):
        pl.semaphore_signal(barrier, inc=1, device_id={"tm": lax.rem(me + d, tm)}, device_id_type=pl.DeviceIdType.MESH)
        return c

    def greet_f(d, c):
        pl.semaphore_signal(barrier, inc=1, device_id={"freq": lax.rem(mf + d, nf)}, device_id_type=pl.DeviceIdType.MESH)
        return c

    lax.fori_loop(1, tm, greet_tm, 0)
    lax.fori_loop(1, nf, greet_f, 0)
    pl.semaphore_wait(barrier, tm + nf - 2)

    def y_copy(j):
        return pltpu.make_async_remote_copy(
            src_ref=ysend.at[j], dst_ref=yrecv.at[me], send_sem=ys_sem.at[j], recv_sem=yr_sem.at[me],
            device_id={"tm": j}, device_id_type=pl.DeviceIdType.MESH)

    def y_from(s):
        return pltpu.make_async_remote_copy(
            src_ref=ysend.at[s], dst_ref=yrecv.at[s], send_sem=ys_sem.at[s], recv_sem=yr_sem.at[s],
            device_id={"tm": s}, device_id_type=pl.DeviceIdType.MESH)

    def s_copy(j):
        return pltpu.make_async_remote_copy(
            src_ref=ssend.at[j], dst_ref=srecv.at[me], send_sem=ss_sem.at[j], recv_sem=sr_sem.at[me],
            device_id={"tm": j}, device_id_type=pl.DeviceIdType.MESH)

    def s_from(s):
        return pltpu.make_async_remote_copy(
            src_ref=ssend.at[s], dst_ref=srecv.at[s], send_sem=ss_sem.at[s], recv_sem=sr_sem.at[s],
            device_id={"tm": s}, device_id_type=pl.DeviceIdType.MESH)

    def k_copy(m, j):
        return pltpu.make_async_remote_copy(
            src_ref=skysend.at[m, j], dst_ref=skyrecv.at[m, mf], send_sem=ks_sem.at[m, j], recv_sem=kr_sem.at[m, mf],
            device_id={"freq": j}, device_id_type=pl.DeviceIdType.MESH)

    def k_from(m, s):
        return pltpu.make_async_remote_copy(
            src_ref=skysend.at[m, s], dst_ref=skyrecv.at[m, s], send_sem=ks_sem.at[m, s], recv_sem=kr_sem.at[m, s],
            device_id={"freq": s}, device_id_type=pl.DeviceIdType.MESH)

    g_copy.wait()
    nt = (((1,), (1,)), ((), ()))

    def project(j):
        vis_copy(j).wait()
        y2 = lax.dot_general(gb[:, :window], visb[j, 0], nt, preferred_element_type=F32)
        y2 = y2 + lax.dot_general(gb[:, window:], visb[j, 1], nt, preferred_element_type=F32)
        y = y2[:2 * RANK] + y2[2 * RANK:]
        strong = y[:2 * len(STRONG)]
        low = strong - strong.astype(BF16).astype(F32)
        return jnp.concatenate([y, low], 0).astype(BF16)

    def send_y(d, c):
        j = lax.rem(me + d, tm)
        ysend[j] = project(j)
        y_copy(j).start()
        return c

    lax.fori_loop(1, tm, send_y, 0)
    yrecv[me] = project(me)

    kl_copy.wait()

    def spread(m, c):
        zero = jnp.zeros((klb.shape[1], 128 - band), BF16)
        for s in range(nf):
            klp[m, :, s * 128:(s + 1) * 128] = jnp.concatenate([klb[m, :, s * band:(s + 1) * band], zero], 1)
        return c

    lax.fori_loop(0, modes, spread, 0)

    lane = lax.broadcasted_iota(jnp.int32, (1, lanes), 1) // band
    share = lanes // band
    count = jnp.zeros((1, lanes), F32)
    for i in range(share):
        count = jnp.where(lane == i, counts[me * share + i].astype(F32), count)
    factor = jnp.sqrt(count) * (1.0 / math.sqrt(128.0 * total))

    e_copy.wait()

    def wait_y(d, c):
        y_from(lax.rem(me + tm - d, tm)).wait_recv()
        return c

    lax.fori_loop(1, tm, wait_y, 0)
    parts = []
    for h in range(2):
        y = yrecv[:, :, h * half:(h + 1) * half].reshape(tm * ROWS, half)
        x = jnp.dot(eb[...], y, preferred_element_type=F32)
        n = x.shape[0] // 2
        parts.append((x[:n] + x[n:]) * factor[:, h * half:(h + 1) * half])
    mq = 2 * modes
    for j in range(tm):
        ssend[j] = jnp.concatenate([p[j * mq:(j + 1) * mq] for p in parts], 0).astype(BF16)

    def send_s(d, c):
        s_copy(lax.rem(me + d, tm)).start()
        return c

    lax.fori_loop(1, tm, send_s, 0)
    srecv[me] = ssend[me]

    def wait_s(d, c):
        s_from(lax.rem(me + tm - d, tm)).wait_recv()
        return c

    lax.fori_loop(1, tm, wait_s, 0)

    stacks = tm * share
    quarter = share // 2

    def unpack(s, c):
        x = srecv[s].astype(F32)
        zero = jnp.zeros((2 * mq, 128 - band), F32)
        for b in range(quarter):
            piece = jnp.concatenate([x[:, b * band:(b + 1) * band], zero], 1)
            for h in range(2):
                wf[pl.ds(s * share + h * quarter + b, mq, stride=stacks), :] = piece[h * mq:(h + 1) * mq]
        return c

    lax.fori_loop(0, tm, unpack, 0)
    for m in range(modes):
        s0 = wf[2 * m * stacks:(2 * m + 1) * stacks]
        s1 = wf[(2 * m + 1) * stacks:(2 * m + 2) * stacks]
        wmat[m, :stacks] = jnp.concatenate([s0, s1], 1).astype(BF16)
        wmat[m, stacks:] = jnp.concatenate([-s1, s0], 1).astype(BF16)

    sky_rows = beamb.shape[3]
    group = 8
    column = lax.broadcasted_iota(jnp.int32, (sky_rows, 256), 1) % 128
    rows_out = sky_rows // nf

    def one_mode(m, c):
        beam_copy(m).wait()

        def some(i, acc):
            x = beamb[m, pl.ds(i * group, group)]
            x = jnp.concatenate([x[:, 0], x[:, 1]], 2).reshape(group * sky_rows, 2 * stacks)
            z = jnp.dot(x, wmat[m], preferred_element_type=F32)
            for f in range(group):
                acc = jnp.where(column == i * group + f, z[f * sky_rows:(f + 1) * sky_rows], acc)
            return acc

        acc = lax.fori_loop(0, band // group, some, jnp.zeros((sky_rows, 256), F32))
        for j in range(nf):
            rows = acc[j * rows_out:(j + 1) * rows_out]
            skysend[m, j] = jnp.concatenate([rows[:, :128], rows[:, 128:]], 0).astype(BF16)

        def send_k(d, c):
            k_copy(m, lax.rem(mf + d, nf)).start()
            return c

        lax.fori_loop(1, nf, send_k, 0)
        skyrecv[m, mf] = skysend[m, mf]
        return c

    lax.fori_loop(0, modes, one_mode, 0)

    def filter_mode(m, c):
        def wait_k(d, c):
            k_from(m, lax.rem(mf + nf - d, nf)).wait_recv()
            return c

        lax.fori_loop(1, nf, wait_k, 0)
        rows = jnp.concatenate([skyrecv[m, s] for s in range(nf)], 1)
        out[m] = lax.dot_general(rows, klp[m], nt, preferred_element_type=F32).astype(BF16)
        return c

    lax.fori_loop(0, modes, filter_mode, 0)

    def drain_tm(d, c):
        j = lax.rem(me + d, tm)
        y_copy(j).wait_send()
        s_copy(j).wait_send()
        return c

    lax.fori_loop(1, tm, drain_tm, 0)

    def drain_f(d, c):
        j = lax.rem(mf + d, nf)
        for m in range(modes):
            k_copy(m, j).wait_send()
        return c

    lax.fori_loop(1, nf, drain_f, 0)


def local(visibilities, counts, beam_inverse, kl_modes):
    tm = lax.axis_size("tm")
    nf = lax.axis_size("freq")
    _, stacks, band, window = visibilities.shape
    modes, _, _, sky_rows, _ = beam_inverse.shape
    kept = kl_modes.shape[1]
    share = stacks // tm
    lanes = share * band
    g, e = factors(modes * tm, window, tm)
    any_space = pl.BlockSpec(memory_space=pl.ANY)
    rows_out = sky_rows // nf
    dma = pltpu.SemaphoreType.DMA
    filtered = pl.pallas_call(
        functools.partial(kernel, tm=tm, nf=nf, total=window * tm),
        out_shape=jax.ShapeDtypeStruct((modes, 2 * rows_out, kept), BF16),
        in_specs=[pl.BlockSpec(memory_space=pltpu.SMEM)] + [any_space] * 5,
        out_specs=pl.BlockSpec(memory_space=pltpu.VMEM),
        scratch_shapes=[
            pltpu.VMEM((tm, 2, lanes, window), BF16),
            pltpu.VMEM(beam_inverse.shape, BF16),
            pltpu.VMEM(kl_modes.shape, BF16),
            pltpu.VMEM((modes, kept, nf * 128), BF16),
            pltpu.VMEM(g.shape, BF16),
            pltpu.VMEM(e.shape, BF16),
            pltpu.VMEM((tm, ROWS, lanes), BF16),
            pltpu.VMEM((tm, ROWS, lanes), BF16),
            pltpu.VMEM((tm, 4 * modes, lanes // 2), BF16),
            pltpu.VMEM((tm, 4 * modes, lanes // 2), BF16),
            pltpu.VMEM((2 * modes * stacks, 128), F32),
            pltpu.VMEM((modes, 2 * stacks, 256), BF16),
            pltpu.VMEM((modes, nf, 2 * rows_out, 128), BF16),
            pltpu.VMEM((modes, nf, 2 * rows_out, 128), BF16),
            dma((tm,)), dma((modes,)), dma((3,)),
            dma((tm,)), dma((tm,)), dma((tm,)), dma((tm,)),
            dma((modes, nf)), dma((modes, nf)),
        ],
        compiler_params=pltpu.CompilerParams(
            collective_id=0, has_side_effects=True, vmem_limit_bytes=56 * 2**20),
    )(counts, visibilities.reshape(2, tm, lanes, window), beam_inverse, kl_modes, jnp.asarray(g), jnp.asarray(e))
    return filtered.reshape(modes, 2, rows_out, kept).transpose(2, 0, 1, 3)


def solution(mesh):
    in_specs = (
        P(None, None, "freq", "tm"),
        P(),
        P("tm", "freq", None, None, None),
        P("tm", None, None),
    )
    out_specs = P("freq", "tm", None, None)
    return jax.shard_map(local, mesh=mesh, in_specs=in_specs, out_specs=out_specs, check_vma=False)
```

```python
import functools
import math

import jax
import jax.numpy as jnp
import ml_dtypes
import numpy as np
from jax import lax
from jax.experimental import pallas as pl
from jax.experimental.pallas import tpu as pltpu
from jax.sharding import PartitionSpec as P

RANK = 12
STRONG = (2, 3, 4, 5)
ROWS = 2 * RANK + 2 * len(STRONG)
F32 = jnp.float32
BF16 = jnp.bfloat16


def window_factors(modes, window, windows):
    total = window * windows
    step = 2.0 * math.pi / total
    m = np.arange(modes, dtype=np.float64)
    t = np.arange(window, dtype=np.float64)
    mc, tc = (modes - 1) / 2.0, (window - 1) / 2.0
    diag = -np.cos(math.pi * (2 * t + 1 - window) / total) * math.cos(math.pi * modes / total)
    off = np.sin(math.pi * (t[:-1] + 1) / total) * np.sin(math.pi * (window - 1 - t[:-1]) / total)
    _, vectors = np.linalg.eigh(np.diag(diag) + np.diag(off, 1) + np.diag(off, -1))
    return m, t, mc, tc, step, vectors


def prolate(modes, window, windows):
    m, t, mc, tc, step, vectors = window_factors(modes, window, windows)
    centred = np.exp(-1j * step * np.outer(m - mc, t - tc))
    strength = np.linalg.norm(centred @ vectors, axis=0)
    basis = vectors[:, np.argsort(-strength)[:RANK]].T
    basis = basis * np.sign(basis[:, :window // 3].sum(1))[:, None]
    expand = centred @ basis.T
    project = basis * np.exp(-1j * step * mc * (t - tc))[None]
    return m, tc, step, expand, project


def halves(x):
    x = np.round(x * 2.0**22) / 2.0**22
    high = x.astype(np.float32).astype(ml_dtypes.bfloat16)
    low = (x - high.astype(np.float64)).astype(np.float32).astype(ml_dtypes.bfloat16)
    return np.concatenate([high, low], 0)


def factors(modes, window, windows):
    m, tc, step, expand, project = prolate(modes, window, windows)
    order = list(STRONG) + [k for k in range(RANK) if k not in STRONG]
    lead = len(STRONG)
    rows = [(k, part) for part in (0, 1) for k in order[:lead]]
    rows += [(k, part) for part in (0, 1) for k in order[lead:]]
    g = np.zeros((2 * RANK, 2, window))
    for at, (k, part) in enumerate(rows):
        re, im = project[k].real, project[k].imag
        g[at] = (re, -im) if part == 0 else (im, re)
    e = np.zeros((modes, 2, windows, ROWS))
    for w in range(windows):
        turned = expand * np.exp(-1j * step * m * (w * window + tc))[:, None]
        for at, (k, part) in enumerate(rows):
            re, im = turned[:, k].real, turned[:, k].imag
            e[:, 0, w, at] = re if part == 0 else -im
            e[:, 1, w, at] = im if part == 0 else re
    e[..., 2 * RANK:] = e[..., :2 * lead]
    return halves(g.reshape(2 * RANK, 2 * window)), halves(e.reshape(2 * modes, windows * ROWS))


def kernel(
    counts, vis, beam, kl, g, e, out,
    visb, beamb, klb, klp, gb, eb, ysend, yrecv, ssend, srecv, wf, wmat, skysend, skyrecv,
    vis_sem, beam_sem, misc_sem, ys_sem, yr_sem, ss_sem, sr_sem, ks_sem, kr_sem,
    *, tm, nf, total,
):
    me = lax.axis_index("tm")
    mf = lax.axis_index("freq")
    lanes = visb.shape[2]
    half = lanes // 2
    modes = beamb.shape[0]
    band = beamb.shape[1]
    window = visb.shape[3]

    g_copy = pltpu.make_async_copy(g, gb, misc_sem.at[0])
    e_copy = pltpu.make_async_copy(e, eb, misc_sem.at[1])
    kl_copy = pltpu.make_async_copy(kl, klb, misc_sem.at[2])
    barrier = pltpu.get_barrier_semaphore()

    per_x = tm // 4
    offsets = [(dx, dr) for dr in range(per_x - 1, -1, -1) for dx in (2, 1, 3, 0) if (dx, dr) != (0, 0)]

    def at(dx, dr):
        x, r = me // per_x, me % per_x
        y, c = r // 2, r % 2
        y, c = lax.rem(y + dr // 2, 2), lax.rem(c + dr % 2, 2)
        return lax.rem(x + dx, 4) * per_x + y * 2 + c

    others = [at(dx, dr) for dx, dr in offsets]
    bands = [lax.rem(mf + d, nf) for d in (4, 5, 3, 6, 2, 7, 1)]
    for j in others:
        pl.semaphore_signal(barrier, inc=1, device_id={"tm": j}, device_id_type=pl.DeviceIdType.MESH)
    for j in bands:
        pl.semaphore_signal(barrier, inc=1, device_id={"freq": j}, device_id_type=pl.DeviceIdType.MESH)
    g_copy.start()

    def vis_copy(j):
        return pltpu.make_async_copy(vis.at[:, j], visb.at[j], vis_sem.at[j])

    def beam_copy(m):
        return pltpu.make_async_copy(beam.at[m], beamb.at[m], beam_sem.at[m])

    def start_vis(j, c):
        vis_copy(j).start()
        return c

    lax.fori_loop(0, tm, start_vis, 0)

    def y_copy(j):
        return pltpu.make_async_remote_copy(
            src_ref=ysend.at[j], dst_ref=yrecv.at[me], send_sem=ys_sem.at[j], recv_sem=yr_sem.at[me],
            device_id={"tm": j}, device_id_type=pl.DeviceIdType.MESH)

    def y_from(s):
        return pltpu.make_async_remote_copy(
            src_ref=ysend.at[s], dst_ref=yrecv.at[s], send_sem=ys_sem.at[s], recv_sem=yr_sem.at[s],
            device_id={"tm": s}, device_id_type=pl.DeviceIdType.MESH)

    def s_copy(j):
        return pltpu.make_async_remote_copy(
            src_ref=ssend.at[j], dst_ref=srecv.at[me], send_sem=ss_sem.at[j], recv_sem=sr_sem.at[me],
            device_id={"tm": j}, device_id_type=pl.DeviceIdType.MESH)

    def s_from(s):
        return pltpu.make_async_remote_copy(
            src_ref=ssend.at[s], dst_ref=srecv.at[s], send_sem=ss_sem.at[s], recv_sem=sr_sem.at[s],
            device_id={"tm": s}, device_id_type=pl.DeviceIdType.MESH)

    def k_copy(m, j):
        return pltpu.make_async_remote_copy(
            src_ref=skysend.at[m, j], dst_ref=skyrecv.at[m, mf], send_sem=ks_sem.at[m, j], recv_sem=kr_sem.at[m, mf],
            device_id={"freq": j}, device_id_type=pl.DeviceIdType.MESH)

    def k_from(m, s):
        return pltpu.make_async_remote_copy(
            src_ref=skysend.at[m, s], dst_ref=skyrecv.at[m, s], send_sem=ks_sem.at[m, s], recv_sem=kr_sem.at[m, s],
            device_id={"freq": s}, device_id_type=pl.DeviceIdType.MESH)

    g_copy.wait()
    nt = (((1,), (1,)), ((), ()))

    def project(j):
        vis_copy(j).wait()
        y2 = lax.dot_general(gb[:, :window], visb[j, 0], nt, preferred_element_type=F32)
        y2 = y2 + lax.dot_general(gb[:, window:], visb[j, 1], nt, preferred_element_type=F32)
        y = y2[:2 * RANK] + y2[2 * RANK:]
        strong = y[:2 * len(STRONG)]
        low = strong - strong.astype(BF16).astype(F32)
        return jnp.concatenate([y, low], 0).astype(BF16)

    def two(i, c):
        for j in (2 * i, 2 * i + 1):
            ysend[j] = project(j)
        return c

    lax.fori_loop(0, tm // 2, two, 0)
    pl.semaphore_wait(barrier, tm + nf - 2)
    for j in others:
        y_copy(j).start()
    yrecv[me] = ysend[me]
    e_copy.start()
    kl_copy.start()
    for m in range(modes):
        beam_copy(m).start()

    kl_copy.wait()

    def spread(m, c):
        zero = jnp.zeros((klb.shape[1], 128 - band), BF16)
        for s in range(nf):
            klp[m, :, s * 128:(s + 1) * 128] = jnp.concatenate([klb[m, :, s * band:(s + 1) * band], zero], 1)
        return c

    lax.fori_loop(0, modes, spread, 0)

    lane = lax.broadcasted_iota(jnp.int32, (1, lanes), 1) // band
    share = lanes // band
    count = jnp.zeros((1, lanes), F32)
    for i in range(share):
        count = jnp.where(lane == i, counts[me * share + i].astype(F32), count)
    factor = jnp.sqrt(count) * (1.0 / math.sqrt(128.0 * total))

    e_copy.wait()
    for j in others:
        y_from(j).wait_recv()
    parts = []
    for h in range(2):
        y = yrecv[:, :, h * half:(h + 1) * half].reshape(tm * ROWS, half)
        x = jnp.dot(eb[...], y, preferred_element_type=F32)
        n = x.shape[0] // 2
        parts.append((x[:n] + x[n:]) * factor[:, h * half:(h + 1) * half])
    mq = 2 * modes
    for j in range(tm):
        ssend[j] = jnp.concatenate([p[j * mq:(j + 1) * mq] for p in parts], 0).astype(BF16)

    for j in others:
        s_copy(j).start()
    srecv[me] = ssend[me]

    for j in others:
        s_from(j).wait_recv()

    stacks = tm * share
    quarter = share // 2

    def unpack(s, c):
        x = srecv[s].astype(F32)
        zero = jnp.zeros((2 * mq, 128 - band), F32)
        for b in range(quarter):
            piece = jnp.concatenate([x[:, b * band:(b + 1) * band], zero], 1)
            for h in range(2):
                wf[pl.ds(s * share + h * quarter + b, mq, stride=stacks), :] = piece[h * mq:(h + 1) * mq]
        return c

    lax.fori_loop(0, tm, unpack, 0)
    for m in range(modes):
        s0 = wf[2 * m * stacks:(2 * m + 1) * stacks]
        s1 = wf[(2 * m + 1) * stacks:(2 * m + 2) * stacks]
        wmat[m, :stacks] = jnp.concatenate([s0, s1], 1).astype(BF16)
        wmat[m, stacks:] = jnp.concatenate([-s1, s0], 1).astype(BF16)

    sky_rows = beamb.shape[3]
    column = lax.broadcasted_iota(jnp.int32, (sky_rows, 256), 1) % 128
    rows_out = sky_rows // nf

    def one_mode(m, c):
        beam_copy(m).wait()

        x = beamb[m]
        x = jnp.concatenate([x[:, 0], x[:, 1]], 2).reshape(band * sky_rows, 2 * stacks)
        z = jnp.dot(x, wmat[m], preferred_element_type=F32)
        acc = jnp.zeros((sky_rows, 256), F32)
        for f in range(band):
            acc = jnp.where(column == f, z[f * sky_rows:(f + 1) * sky_rows], acc)
        for j in range(nf):
            rows = acc[j * rows_out:(j + 1) * rows_out]
            skysend[m, j] = jnp.concatenate([rows[:, :128], rows[:, 128:]], 0).astype(BF16)

        for j in bands:
            k_copy(m, j).start()
        skyrecv[m, mf] = skysend[m, mf]
        return c

    lax.fori_loop(0, modes, one_mode, 0)

    def filter_mode(m, c):
        for j in bands:
            k_from(m, j).wait_recv()
        rows = jnp.concatenate([skyrecv[m, s] for s in range(nf)], 1)
        out[m] = lax.dot_general(rows, klp[m], nt, preferred_element_type=F32).astype(BF16)
        return c

    lax.fori_loop(0, modes, filter_mode, 0)

    for j in others:
        y_copy(j).wait_send()
        s_copy(j).wait_send()
    for j in bands:
        for m in range(modes):
            k_copy(m, j).wait_send()


def local(visibilities, counts, beam_inverse, kl_modes):
    tm = lax.axis_size("tm")
    nf = lax.axis_size("freq")
    _, stacks, band, window = visibilities.shape
    modes, _, _, sky_rows, _ = beam_inverse.shape
    kept = kl_modes.shape[1]
    share = stacks // tm
    lanes = share * band
    g, e = factors(modes * tm, window, tm)
    any_space = pl.BlockSpec(memory_space=pl.ANY)
    rows_out = sky_rows // nf
    dma = pltpu.SemaphoreType.DMA
    filtered = pl.pallas_call(
        functools.partial(kernel, tm=tm, nf=nf, total=window * tm),
        out_shape=jax.ShapeDtypeStruct((modes, 2 * rows_out, kept), BF16),
        in_specs=[pl.BlockSpec(memory_space=pltpu.SMEM)] + [any_space] * 5,
        out_specs=pl.BlockSpec(memory_space=pltpu.VMEM),
        scratch_shapes=[
            pltpu.VMEM((tm, 2, lanes, window), BF16),
            pltpu.VMEM(beam_inverse.shape, BF16),
            pltpu.VMEM(kl_modes.shape, BF16),
            pltpu.VMEM((modes, kept, nf * 128), BF16),
            pltpu.VMEM(g.shape, BF16),
            pltpu.VMEM(e.shape, BF16),
            pltpu.VMEM((tm, ROWS, lanes), BF16),
            pltpu.VMEM((tm, ROWS, lanes), BF16),
            pltpu.VMEM((tm, 4 * modes, lanes // 2), BF16),
            pltpu.VMEM((tm, 4 * modes, lanes // 2), BF16),
            pltpu.VMEM((2 * modes * stacks, 128), F32),
            pltpu.VMEM((modes, 2 * stacks, 256), BF16),
            pltpu.VMEM((modes, nf, 2 * rows_out, 128), BF16),
            pltpu.VMEM((modes, nf, 2 * rows_out, 128), BF16),
            dma((tm,)), dma((modes,)), dma((3,)),
            dma((tm,)), dma((tm,)), dma((tm,)), dma((tm,)),
            dma((modes, nf)), dma((modes, nf)),
        ],
        compiler_params=pltpu.CompilerParams(
            collective_id=0, has_side_effects=True, vmem_limit_bytes=56 * 2**20),
    )(counts, visibilities.reshape(2, tm, lanes, window), beam_inverse, kl_modes, jnp.asarray(g), jnp.asarray(e))
    return filtered.reshape(modes, 2, rows_out, kept).transpose(2, 0, 1, 3)


def solution(mesh):
    in_specs = (
        P(None, None, "freq", "tm"),
        P(),
        P("tm", "freq", None, None, None),
        P("tm", None, None),
    )
    out_specs = P("freq", "tm", None, None)
    return jax.shard_map(local, mesh=mesh, in_specs=in_specs, out_specs=out_specs, check_vma=False)
```

```python
import functools
import math

import jax
import jax.numpy as jnp
import ml_dtypes
import numpy as np
from jax import lax
from jax.experimental import pallas as pl
from jax.experimental.pallas import tpu as pltpu
from jax.sharding import PartitionSpec as P

RANK = 17
STRONG = (7, 8, 9)
DATA = 2 * RANK
ROWS = DATA + 2 * len(STRONG)
SUMS = 40
AHEAD = 4
GREETED = 4
KNOWN = 3
F32 = jnp.float32
BF16 = jnp.bfloat16


def window_factors(modes, window, windows):
    total = window * windows
    step = 2.0 * math.pi / total
    m = np.arange(modes, dtype=np.float64)
    t = np.arange(window, dtype=np.float64)
    mc, tc = (modes - 1) / 2.0, (window - 1) / 2.0
    diag = -np.cos(math.pi * (2 * t + 1 - window) / total) * math.cos(math.pi * modes / total)
    off = np.sin(math.pi * (t[:-1] + 1) / total) * np.sin(math.pi * (window - 1 - t[:-1]) / total)
    _, vectors = np.linalg.eigh(np.diag(diag) + np.diag(off, 1) + np.diag(off, -1))
    return m, t, mc, tc, step, vectors


def prolate(modes, window, windows):
    m, t, mc, tc, step, vectors = window_factors(modes, window, windows)
    centred = np.exp(-1j * step * np.outer(m - mc, t - tc))
    strength = np.linalg.norm(centred @ vectors, axis=0)
    basis = vectors[:, np.argsort(-strength)[:RANK]].T
    basis = basis * np.sign(basis[:, :window // 3].sum(1))[:, None]
    expand = centred @ basis.T
    project = basis * np.exp(-1j * step * mc * (t - tc))[None]
    return m, tc, step, expand, project


def halves(x):
    x = np.round(x * 2.0**22) / 2.0**22
    high = x.astype(np.float32).astype(ml_dtypes.bfloat16)
    low = (x - high.astype(np.float64)).astype(np.float32).astype(ml_dtypes.bfloat16)
    return np.concatenate([high, low], 0)


def factors(modes, window, windows):
    m, tc, step, expand, project = prolate(modes, window, windows)
    weak = [(k, part) for part in (0, 1) for k in range(RANK) if k not in STRONG]
    strong = [(k, part) for part in (0, 1) for k in STRONG]
    lead = DATA - 32
    rows = weak[:lead] + strong + weak[lead:]
    g = np.zeros((SUMS, 2, window))
    for at, (k, part) in enumerate(rows):
        re, im = project[k].real, project[k].imag
        g[at] = (re, -im) if part == 0 else (im, re)
    e = np.zeros((modes, 2, windows, ROWS))
    for w in range(windows):
        turned = expand * np.exp(-1j * step * m * (w * window + tc))[:, None]
        for at, (k, part) in enumerate(rows):
            re, im = turned[:, k].real, turned[:, k].imag
            e[:, 0, w, at] = re if part == 0 else -im
            e[:, 1, w, at] = im if part == 0 else re
    e[..., DATA:] = e[..., lead:lead + 2 * len(STRONG)]
    g = g.reshape(SUMS, 2, 2, window // 2).transpose(2, 0, 1, 3)
    g = np.stack([halves(core.reshape(SUMS, window)) for core in g])
    return g, halves(e.reshape(2 * modes, windows * ROWS))


def kernel(
    countsh, vis, beam, kl, g, e, out,
    counts, visb, beamb, klb, klp, gb, eb, pairsend, pairrecv, ysend, yrecv, ssend, srecv, wf, wmat, skysend, skyrecv,
    vis_sem, beam_sem, misc_sem, ps_sem, pr_sem, x_sem, z_sem, ys_sem, yr_sem, ss_sem, sr_sem, ks_sem, kr_sem,
    *, tm, nf, total,
):
    me = lax.axis_index("tm")
    mf = lax.axis_index("freq")
    lanes = visb.shape[2]
    half = lanes // 2
    modes = beamb.shape[0]
    band = beamb.shape[1]
    window = visb.shape[3]

    core = me % 2
    chip = me // 2
    chips = tm // 2
    g_copy = pltpu.make_async_copy(g.at[core], gb, misc_sem.at[0])
    e_copy = pltpu.make_async_copy(e, eb, misc_sem.at[1])
    kl_copy = pltpu.make_async_copy(kl, klb, misc_sem.at[2])
    count_copy = pltpu.make_async_copy(countsh, counts, misc_sem.at[3])
    barrier = pltpu.get_barrier_semaphore()

    def at(dx, dy, dc):
        x, y = chip // 2, chip % 2
        return lax.rem(x + dx, chips // 2) * 4 + lax.rem(y + dy, 2) * 2 + lax.rem(core + dc, 2)

    steps = [(dx, dy) for dy in (1, 0) for dx in (2, 1, 3, 0) if (dx, dy) != (0, 0)]
    near = [(0, 1), (2, 0), (1, 0), (3, 0)]
    far = [(2, 1), (1, 1), (3, 1)]
    same = [at(dx, dy, 0) for dx, dy in far + near]
    chip_order = [j // 2 for j in same] + [chip]
    partner = at(0, 0, 1)
    others = [at(dx, dy, dc) for dx, dy in steps for dc in (1, 0)] + [partner]
    along_x = [at(dx, 0, 0) for dx in (2, 1, 3)]
    across = at(0, 1, 0)
    z, low_y = mf // 2, mf % 2
    along_z = [lax.rem(z + dz, nf // 2) * 2 + low_y for dz in (2, 1, 3)]
    beside = z * 2 + 1 - low_y
    bands = [lax.rem(z + dz, nf // 2) * 2 + lax.rem(low_y + dy, 2) for dy in (1, 0) for dz in (2, 1, 3)] + [beside]

    def signal(sem, **where):
        pl.semaphore_signal(sem, inc=1, device_id=where, device_id_type=pl.DeviceIdType.MESH)

    for j in along_x + [across, partner]:
        signal(barrier, tm=j)
    for j in along_z + [beside]:
        signal(barrier, freq=j)
    g_copy.start()

    def vis_copy(j):
        return pltpu.make_async_copy(vis.at[:, j], visb.at[j], vis_sem.at[j])

    def beam_copy(m):
        return pltpu.make_async_copy(beam.at[m], beamb.at[m], beam_sem.at[m])

    def chunk(k):
        return 2 * chip_order[k % chips] + (1 - core if k < chips else core)

    for k in range(AHEAD):
        vis_copy(chunk(k)).start()
    count_copy.start()

    def pair_copy(i):
        return pltpu.make_async_remote_copy(
            src_ref=pairsend.at[i], dst_ref=pairrecv.at[i], send_sem=ps_sem.at[i], recv_sem=pr_sem.at[i],
            device_id={"tm": partner}, device_id_type=pl.DeviceIdType.MESH)

    def y_copy(k):
        return pltpu.make_async_remote_copy(
            src_ref=ysend.at[k], dst_ref=yrecv.at[chip], send_sem=ys_sem.at[k], recv_sem=yr_sem.at[chip],
            device_id={"tm": same[k]}, device_id_type=pl.DeviceIdType.MESH)

    def y_from(s):
        return pltpu.make_async_remote_copy(
            src_ref=ysend.at[s // 2], dst_ref=yrecv.at[s // 2], send_sem=ys_sem.at[s // 2], recv_sem=yr_sem.at[s // 2],
            device_id={"tm": s}, device_id_type=pl.DeviceIdType.MESH)

    def s_copy(j):
        return pltpu.make_async_remote_copy(
            src_ref=ssend.at[j], dst_ref=srecv.at[me], send_sem=ss_sem.at[j], recv_sem=sr_sem.at[me],
            device_id={"tm": j}, device_id_type=pl.DeviceIdType.MESH)

    def s_from(s):
        return pltpu.make_async_remote_copy(
            src_ref=ssend.at[s], dst_ref=srecv.at[s], send_sem=ss_sem.at[s], recv_sem=sr_sem.at[s],
            device_id={"tm": s}, device_id_type=pl.DeviceIdType.MESH)

    def k_copy(m, j):
        return pltpu.make_async_remote_copy(
            src_ref=skysend.at[m, j], dst_ref=skyrecv.at[m, mf], send_sem=ks_sem.at[m, j], recv_sem=kr_sem.at[m, mf],
            device_id={"freq": j}, device_id_type=pl.DeviceIdType.MESH)

    def k_from(m, s):
        return pltpu.make_async_remote_copy(
            src_ref=skysend.at[m, s], dst_ref=skyrecv.at[m, s], send_sem=ks_sem.at[m, s], recv_sem=kr_sem.at[m, s],
            device_id={"freq": s}, device_id_type=pl.DeviceIdType.MESH)

    nt = (((1,), (1,)), ((), ()))

    def project(k):
        j = chunk(k)
        vis_copy(j).wait()
        if k + AHEAD < tm:
            vis_copy(chunk(k + AHEAD)).start()
        y = lax.dot_general(gb[:, :window], visb[j, 0], nt, preferred_element_type=F32)
        y = y + lax.dot_general(gb[:, window:], visb[j, 1], nt, preferred_element_type=F32)
        return y[:SUMS] + y[SUMS:]

    g_copy.wait()
    for k in range(chips):
        pairsend[k] = project(k)
        if k == GREETED:
            pl.semaphore_wait(barrier, 9)
            for j in along_x:
                signal(x_sem, tm=j)
            for j in along_z:
                signal(z_sem, freq=j)
            for i in range(k):
                pair_copy(i).start()
        if k >= GREETED:
            pair_copy(k).start()
    row = lax.broadcasted_iota(jnp.int32, (ROWS - 32, lanes), 0) + 32

    for k in range(chips):
        own = project(k + chips)
        pair_copy(k).wait_recv()
        y = own + pairrecv[k]
        low = y[:ROWS - 32]
        low = low - low.astype(BF16).astype(F32)
        tail = y[32:]
        if ROWS > SUMS:
            tail = jnp.concatenate([tail, tail[:ROWS - SUMS]], 0)
        y = jnp.concatenate([y[:32], jnp.where(row < DATA, tail, low)], 0)
        y = jnp.concatenate([y[:, :half], y[:, half:]], 0).astype(BF16)
        if k < chips - 1:
            ysend[k] = y
        else:
            yrecv[chip] = y
        if k == KNOWN:
            pl.semaphore_wait(x_sem, 3)
            for i in range(k):
                y_copy(i).start()
        if KNOWN <= k < chips - 1:
            y_copy(k).start()
    e_copy.start()
    kl_copy.start()
    for m in range(modes):
        beam_copy(m).start()

    kl_copy.wait()

    def spread(m, c):
        zero = jnp.zeros((klb.shape[1], 128 - band), BF16)
        for s in range(nf):
            klp[m, :, s * 128:(s + 1) * 128] = jnp.concatenate([klb[m, :, s * band:(s + 1) * band], zero], 1)
        return c

    lax.fori_loop(0, modes, spread, 0)

    lane = lax.broadcasted_iota(jnp.int32, (1, lanes), 1) // band
    share = lanes // band
    count_copy.wait()
    count = jnp.zeros((1, lanes), F32)
    for i in range(share):
        count = jnp.where(lane == i, counts[me * share + i].astype(F32), count)
    factor = jnp.sqrt(count) * (1.0 / math.sqrt(128.0 * total))

    e_copy.wait()
    for j in same:
        y_from(j).wait_recv()
    parts = []
    for h in range(2):
        y = yrecv[:, h * ROWS:(h + 1) * ROWS].reshape(chips * ROWS, half)
        x = jnp.dot(eb[...], y, preferred_element_type=F32)
        n = x.shape[0] // 2
        parts.append((x[:n] + x[n:]) * factor[:, h * half:(h + 1) * half])
    mq = 2 * modes
    for j in range(tm):
        ssend[j] = jnp.concatenate([p[j * mq:(j + 1) * mq] for p in parts], 0).astype(BF16)

    for j in others:
        s_copy(j).start()
    srecv[me] = ssend[me]

    for j in others:
        s_from(j).wait_recv()

    stacks = tm * share
    quarter = share // 2

    def unpack(s, c):
        x = srecv[s].astype(F32)
        zero = jnp.zeros((2 * mq, 128 - band), F32)
        for b in range(quarter):
            piece = jnp.concatenate([x[:, b * band:(b + 1) * band], zero], 1)
            for h in range(2):
                wf[pl.ds(s * share + h * quarter + b, mq, stride=stacks), :] = piece[h * mq:(h + 1) * mq]
        return c

    lax.fori_loop(0, tm, unpack, 0)
    for m in range(modes):
        s0 = wf[2 * m * stacks:(2 * m + 1) * stacks]
        s1 = wf[(2 * m + 1) * stacks:(2 * m + 2) * stacks]
        wmat[m, :stacks] = jnp.concatenate([s0, s1], 1).astype(BF16)
        wmat[m, stacks:] = jnp.concatenate([-s1, s0], 1).astype(BF16)

    pl.semaphore_wait(z_sem, 3)

    sky_rows = beamb.shape[3]
    column = lax.broadcasted_iota(jnp.int32, (sky_rows, 256), 1) % 128
    rows_out = sky_rows // nf

    def one_mode(m, c):
        beam_copy(m).wait()

        x = beamb[m]
        x = jnp.concatenate([x[:, 0], x[:, 1]], 2).reshape(band * sky_rows, 2 * stacks)
        z = jnp.dot(x, wmat[m], preferred_element_type=F32)
        acc = jnp.zeros((sky_rows, 256), F32)
        for f in range(band):
            acc = jnp.where(column == f, z[f * sky_rows:(f + 1) * sky_rows], acc)
        for j in range(nf):
            rows = acc[j * rows_out:(j + 1) * rows_out]
            skysend[m, j] = jnp.concatenate([rows[:, :128], rows[:, 128:]], 0).astype(BF16)

        for j in bands:
            k_copy(m, j).start()
        skyrecv[m, mf] = skysend[m, mf]
        return c

    lax.fori_loop(0, modes, one_mode, 0)

    def filter_mode(m, c):
        for j in bands:
            k_from(m, j).wait_recv()
        rows = jnp.concatenate([skyrecv[m, s] for s in range(nf)], 1)
        out[m] = lax.dot_general(rows, klp[m], nt, preferred_element_type=F32).astype(BF16)
        return c

    lax.fori_loop(0, modes, filter_mode, 0)

    lax.fori_loop(0, chips, lambda i, c: (pair_copy(i).wait_send(), c)[1], 0)
    for k in range(chips - 1):
        y_copy(k).wait_send()
    for j in others:
        s_copy(j).wait_send()
    for j in bands:
        for m in range(modes):
            k_copy(m, j).wait_send()


def local(visibilities, counts, beam_inverse, kl_modes):
    tm = lax.axis_size("tm")
    nf = lax.axis_size("freq")
    _, stacks, band, window = visibilities.shape
    modes, _, _, sky_rows, _ = beam_inverse.shape
    kept = kl_modes.shape[1]
    share = stacks // tm
    lanes = share * band
    g, e = factors(modes * tm, 2 * window, tm // 2)
    any_space = pl.BlockSpec(memory_space=pl.ANY)
    rows_out = sky_rows // nf
    dma = pltpu.SemaphoreType.DMA
    filtered = pl.pallas_call(
        functools.partial(kernel, tm=tm, nf=nf, total=window * tm),
        out_shape=jax.ShapeDtypeStruct((modes, 2 * rows_out, kept), BF16),
        in_specs=[any_space] * 6,
        out_specs=pl.BlockSpec(memory_space=pltpu.VMEM),
        scratch_shapes=[
            pltpu.SMEM(counts.shape, jnp.int32),
            pltpu.VMEM((tm, 2, lanes, window), BF16),
            pltpu.VMEM(beam_inverse.shape, BF16),
            pltpu.VMEM(kl_modes.shape, BF16),
            pltpu.VMEM((modes, kept, nf * 128), BF16),
            pltpu.VMEM(g.shape[1:], BF16),
            pltpu.VMEM(e.shape, BF16),
            pltpu.VMEM((tm // 2, SUMS, lanes), F32),
            pltpu.VMEM((tm // 2, SUMS, lanes), F32),
            pltpu.VMEM((tm // 2, 2 * ROWS, lanes // 2), BF16),
            pltpu.VMEM((tm // 2, 2 * ROWS, lanes // 2), BF16),
            pltpu.VMEM((tm, 4 * modes, lanes // 2), BF16),
            pltpu.VMEM((tm, 4 * modes, lanes // 2), BF16),
            pltpu.VMEM((2 * modes * stacks, 128), F32),
            pltpu.VMEM((modes, 2 * stacks, 256), BF16),
            pltpu.VMEM((modes, nf, 2 * rows_out, 128), BF16),
            pltpu.VMEM((modes, nf, 2 * rows_out, 128), BF16),
            dma((tm,)), dma((modes,)), dma((4,)),
            dma((tm // 2,)), dma((tm // 2,)), pltpu.SemaphoreType.REGULAR, pltpu.SemaphoreType.REGULAR,
            dma((tm // 2,)), dma((tm // 2,)), dma((tm,)), dma((tm,)),
            dma((modes, nf)), dma((modes, nf)),
        ],
        compiler_params=pltpu.CompilerParams(
            collective_id=0, has_side_effects=True, vmem_limit_bytes=56 * 2**20),
    )(counts, visibilities.reshape(2, tm, lanes, window), beam_inverse, kl_modes, jnp.asarray(g), jnp.asarray(e))
    return filtered.reshape(modes, 2, rows_out, kept).transpose(2, 0, 1, 3)


def solution(mesh):
    in_specs = (
        P(None, None, "freq", "tm"),
        P(),
        P("tm", "freq", None, None, None),
        P("tm", None, None),
    )
    out_specs = P("freq", "tm", None, None)
    return jax.shard_map(local, mesh=mesh, in_specs=in_specs, out_specs=out_specs, check_vma=False)
```

```python
import functools
import math

import jax
import jax.numpy as jnp
import ml_dtypes
import numpy as np
from jax import lax
from jax.experimental import pallas as pl
from jax.experimental.pallas import tpu as pltpu
from jax.sharding import PartitionSpec as P

RANK = 17
STRONG = (7, 8, 9)
DATA = 2 * RANK
ROWS = DATA + 2 * len(STRONG)
SUMS = 40
AHEAD = 4
GREETED = 4
KNOWN = 3
F32 = jnp.float32
BF16 = jnp.bfloat16


def window_factors(modes, window, windows):
    total = window * windows
    step = 2.0 * math.pi / total
    m = np.arange(modes, dtype=np.float64)
    t = np.arange(window, dtype=np.float64)
    mc, tc = (modes - 1) / 2.0, (window - 1) / 2.0
    diag = -np.cos(math.pi * (2 * t + 1 - window) / total) * math.cos(math.pi * modes / total)
    off = np.sin(math.pi * (t[:-1] + 1) / total) * np.sin(math.pi * (window - 1 - t[:-1]) / total)
    _, vectors = np.linalg.eigh(np.diag(diag) + np.diag(off, 1) + np.diag(off, -1))
    return m, t, mc, tc, step, vectors


def prolate(modes, window, windows):
    m, t, mc, tc, step, vectors = window_factors(modes, window, windows)
    centred = np.exp(-1j * step * np.outer(m - mc, t - tc))
    strength = np.linalg.norm(centred @ vectors, axis=0)
    basis = vectors[:, np.argsort(-strength)[:RANK]].T
    basis = basis * np.sign(basis[:, :window // 3].sum(1))[:, None]
    expand = centred @ basis.T
    project = basis * np.exp(-1j * step * mc * (t - tc))[None]
    return m, tc, step, expand, project


def halves(x):
    x = np.round(x * 2.0**22) / 2.0**22
    high = x.astype(np.float32).astype(ml_dtypes.bfloat16)
    low = (x - high.astype(np.float64)).astype(np.float32).astype(ml_dtypes.bfloat16)
    return np.concatenate([high, low], 0)


def factors(modes, window, windows):
    m, tc, step, expand, project = prolate(modes, window, windows)
    weak = [(k, part) for part in (0, 1) for k in range(RANK) if k not in STRONG]
    strong = [(k, part) for part in (0, 1) for k in STRONG]
    lead = DATA - 32
    rows = weak[:lead] + strong + weak[lead:]
    g = np.zeros((SUMS, 2, window))
    for at, (k, part) in enumerate(rows):
        re, im = project[k].real, project[k].imag
        g[at] = (re, -im) if part == 0 else (im, re)
    e = np.zeros((modes, 2, windows, ROWS))
    for w in range(windows):
        turned = expand * np.exp(-1j * step * m * (w * window + tc))[:, None]
        for at, (k, part) in enumerate(rows):
            re, im = turned[:, k].real, turned[:, k].imag
            e[:, 0, w, at] = re if part == 0 else -im
            e[:, 1, w, at] = im if part == 0 else re
    e[..., DATA:] = e[..., lead:lead + 2 * len(STRONG)]
    g = g.reshape(SUMS, 2, 2, window // 2).transpose(2, 0, 1, 3)
    g = np.stack([halves(core.reshape(SUMS, window)) for core in g])
    return g, halves(e.reshape(2 * modes, windows * ROWS))


def kernel(
    countsh, vis, beam, kl, g, e, out,
    counts, visb, beamb, klb, klp, gb, eb, pairsend, pairrecv, ysend, yrecv, ssend, srecv, wf, wmat, skysend, skyrecv,
    vis_sem, beam_sem, misc_sem, ps_sem, pr_sem, x_sem, z_sem, ys_sem, yr_sem, ss_sem, sr_sem, ks_sem, kr_sem,
    *, tm, nf, total,
):
    me = lax.axis_index("tm")
    mf = lax.axis_index("freq")
    lanes = visb.shape[2]
    half = lanes // 2
    modes = beamb.shape[0]
    band = beamb.shape[1]
    window = visb.shape[3]

    core = me % 2
    chip = me // 2
    chips = tm // 2
    g_copy = pltpu.make_async_copy(g.at[core], gb, misc_sem.at[0])
    e_copy = pltpu.make_async_copy(e, eb, misc_sem.at[1])
    kl_copy = pltpu.make_async_copy(kl, klb, misc_sem.at[2])
    count_copy = pltpu.make_async_copy(countsh, counts, misc_sem.at[3])
    barrier = pltpu.get_barrier_semaphore()

    def at(dx, dy, dc):
        x, y = chip // 2, chip % 2
        return lax.rem(x + dx, chips // 2) * 4 + lax.rem(y + dy, 2) * 2 + lax.rem(core + dc, 2)

    steps = [(dx, dy) for dy in (1, 0) for dx in (2, 1, 3, 0) if (dx, dy) != (0, 0)]
    near = [(0, 1), (2, 0), (1, 0), (3, 0)]
    far = [(2, 1), (1, 1), (3, 1)]
    same = [at(dx, dy, 0) for dx, dy in far + near]
    chip_order = [j // 2 for j in same] + [chip]
    partner = at(0, 0, 1)
    others = [at(dx, dy, dc) for dx, dy in steps for dc in (1, 0)] + [partner]
    along_x = [at(dx, 0, 0) for dx in (2, 1, 3)]
    across = at(0, 1, 0)
    z, low_y = mf // 2, mf % 2
    along_z = [lax.rem(z + dz, nf // 2) * 2 + low_y for dz in (2, 1, 3)]
    beside = z * 2 + 1 - low_y
    bands = [lax.rem(z + dz, nf // 2) * 2 + lax.rem(low_y + dy, 2) for dy in (1, 0) for dz in (2, 1, 3)] + [beside]

    def signal(sem, **where):
        pl.semaphore_signal(sem, inc=1, device_id=where, device_id_type=pl.DeviceIdType.MESH)

    for j in along_x + [across, partner]:
        signal(barrier, tm=j)
    for j in along_z + [beside]:
        signal(barrier, freq=j)
    g_copy.start()

    def vis_copy(j):
        return pltpu.make_async_copy(vis.at[:, j], visb.at[j], vis_sem.at[j])

    def beam_copy(m):
        return pltpu.make_async_copy(beam.at[m], beamb.at[m], beam_sem.at[m])

    def chunk(k):
        return 2 * chip_order[k % chips] + (1 - core if k < chips else core)

    for k in range(AHEAD):
        vis_copy(chunk(k)).start()
    count_copy.start()

    def pair_copy(i):
        return pltpu.make_async_remote_copy(
            src_ref=pairsend.at[i], dst_ref=pairrecv.at[i], send_sem=ps_sem.at[i], recv_sem=pr_sem.at[i],
            device_id={"tm": partner}, device_id_type=pl.DeviceIdType.MESH)

    def y_copy(k):
        return pltpu.make_async_remote_copy(
            src_ref=ysend.at[k], dst_ref=yrecv.at[chip], send_sem=ys_sem.at[k], recv_sem=yr_sem.at[chip],
            device_id={"tm": same[k]}, device_id_type=pl.DeviceIdType.MESH)

    def y_from(s):
        return pltpu.make_async_remote_copy(
            src_ref=ysend.at[s // 2], dst_ref=yrecv.at[s // 2], send_sem=ys_sem.at[s // 2], recv_sem=yr_sem.at[s // 2],
            device_id={"tm": s}, device_id_type=pl.DeviceIdType.MESH)

    def s_copy(j):
        return pltpu.make_async_remote_copy(
            src_ref=ssend.at[j], dst_ref=srecv.at[me], send_sem=ss_sem.at[j], recv_sem=sr_sem.at[me],
            device_id={"tm": j}, device_id_type=pl.DeviceIdType.MESH)

    def s_from(s):
        return pltpu.make_async_remote_copy(
            src_ref=ssend.at[s], dst_ref=srecv.at[s], send_sem=ss_sem.at[s], recv_sem=sr_sem.at[s],
            device_id={"tm": s}, device_id_type=pl.DeviceIdType.MESH)

    def k_copy(m, j):
        return pltpu.make_async_remote_copy(
            src_ref=skysend.at[m, j], dst_ref=skyrecv.at[m, mf], send_sem=ks_sem.at[m, j], recv_sem=kr_sem.at[m, mf],
            device_id={"freq": j}, device_id_type=pl.DeviceIdType.MESH)

    def k_from(m, s):
        return pltpu.make_async_remote_copy(
            src_ref=skysend.at[m, s], dst_ref=skyrecv.at[m, s], send_sem=ks_sem.at[m, s], recv_sem=kr_sem.at[m, s],
            device_id={"freq": s}, device_id_type=pl.DeviceIdType.MESH)

    nt = (((1,), (1,)), ((), ()))

    def project(k):
        j = chunk(k)
        vis_copy(j).wait()
        if k + AHEAD < tm:
            vis_copy(chunk(k + AHEAD)).start()
        y = lax.dot_general(gb[:, :window], visb[j, 0], nt, preferred_element_type=F32)
        y = y + lax.dot_general(gb[:, window:], visb[j, 1], nt, preferred_element_type=F32)
        return y[:SUMS] + y[SUMS:]

    g_copy.wait()
    for k in range(chips):
        pairsend[k] = project(k)
        if k == GREETED:
            pl.semaphore_wait(barrier, 9)
            for j in along_x:
                signal(x_sem, tm=j)
            for j in along_z:
                signal(z_sem, freq=j)
            for i in range(k):
                pair_copy(i).start()
        if k >= GREETED:
            pair_copy(k).start()
    row = lax.broadcasted_iota(jnp.int32, (ROWS - 32, lanes), 0) + 32

    for k in range(chips):
        own = project(k + chips)
        pair_copy(k).wait_recv()
        y = own + pairrecv[k]
        low = y[:ROWS - 32]
        low = low - low.astype(BF16).astype(F32)
        tail = y[32:]
        if ROWS > SUMS:
            tail = jnp.concatenate([tail, tail[:ROWS - SUMS]], 0)
        y = jnp.concatenate([y[:32], jnp.where(row < DATA, tail, low)], 0)
        y = jnp.concatenate([y[:, :half], y[:, half:]], 0).astype(BF16)
        if k < chips - 1:
            ysend[k] = y
        else:
            yrecv[chip] = y
        if k == KNOWN:
            pl.semaphore_wait(x_sem, 3)
            for i in range(k):
                y_copy(i).start()
        if KNOWN <= k < chips - 1:
            y_copy(k).start()
    e_copy.start()
    kl_copy.start()
    for m in range(modes):
        beam_copy(m).start()

    kl_copy.wait()

    def spread(m, c):
        zero = jnp.zeros((klb.shape[1], 128 - band), BF16)
        for s in range(nf):
            klp[m, :, s * 128:(s + 1) * 128] = jnp.concatenate([klb[m, :, s * band:(s + 1) * band], zero], 1)
        return c

    lax.fori_loop(0, modes, spread, 0)

    lane = lax.broadcasted_iota(jnp.int32, (1, lanes), 1) // band
    share = lanes // band
    count_copy.wait()
    count = jnp.zeros((1, lanes), F32)
    for i in range(share):
        count = jnp.where(lane == i, counts[me * share + i].astype(F32), count)
    factor = jnp.sqrt(count) * (1.0 / math.sqrt(128.0 * total))

    e_copy.wait()
    for j in same:
        y_from(j).wait_recv()
    parts = []
    for h in range(2):
        y = yrecv[:, h * ROWS:(h + 1) * ROWS].reshape(chips * ROWS, half)
        x = jnp.dot(eb[...], y, preferred_element_type=F32)
        n = x.shape[0] // 2
        parts.append((x[:n] + x[n:]) * factor[:, h * half:(h + 1) * half])
    mq = 2 * modes
    for j in range(tm):
        ssend[j] = jnp.concatenate([p[j * mq:(j + 1) * mq] for p in parts], 0).astype(BF16)

    for j in others:
        s_copy(j).start()
    srecv[me] = ssend[me]

    for j in others:
        s_from(j).wait_recv()

    stacks = tm * share
    quarter = share // 2

    zero = jnp.zeros((2 * mq, 128 - band), F32)
    def unpack(i, c):
        for s in range(4):
            s = 4 * i + s
            x = srecv[s].astype(F32)
            for b in range(quarter):
                piece = jnp.concatenate([x[:, b * band:(b + 1) * band], zero], 1)
                for h in range(2):
                    wf[pl.ds(s * share + h * quarter + b, mq, stride=stacks), :] = piece[h * mq:(h + 1) * mq]
        return c

    lax.fori_loop(0, tm // 4, unpack, 0)
    for m in range(modes):
        s0 = wf[2 * m * stacks:(2 * m + 1) * stacks]
        s1 = wf[(2 * m + 1) * stacks:(2 * m + 2) * stacks]
        wmat[m, :stacks] = jnp.concatenate([s0, s1], 1).astype(BF16)
        wmat[m, stacks:] = jnp.concatenate([-s1, s0], 1).astype(BF16)

    pl.semaphore_wait(z_sem, 3)

    sky_rows = beamb.shape[3]
    column = lax.broadcasted_iota(jnp.int32, (sky_rows, 256), 1) % 128
    rows_out = sky_rows // nf

    def one_mode(m, c):
        beam_copy(m).wait()
        x = beamb[m]
        x = jnp.concatenate([x[:, 0], x[:, 1]], 2).reshape(band * sky_rows, 2 * stacks)
        z = jnp.dot(x, wmat[m], preferred_element_type=F32)
        acc = jnp.zeros((sky_rows, 256), F32)
        for f in range(band):
            acc = jnp.where(column == f, z[f * sky_rows:(f + 1) * sky_rows], acc)
        for j in range(nf):
            rows = acc[j * rows_out:(j + 1) * rows_out]
            skysend[m, j] = jnp.concatenate([rows[:, :128], rows[:, 128:]], 0).astype(BF16)

        for j in bands:
            k_copy(m, j).start()
        skyrecv[m, mf] = skysend[m, mf]
        return c

    lax.fori_loop(0, modes, one_mode, 0)

    for m in range(modes):
        for j in bands:
            k_from(m, j).wait_recv()
        rows = jnp.concatenate([skyrecv[m, s] for s in range(nf)], 1)
        out[m] = lax.dot_general(rows, klp[m], nt, preferred_element_type=F32).astype(BF16)

    lax.fori_loop(0, chips, lambda i, c: (pair_copy(i).wait_send(), c)[1], 0)
    for k in range(chips - 1):
        y_copy(k).wait_send()
    for j in others:
        s_copy(j).wait_send()
    for j in bands:
        for m in range(modes):
            k_copy(m, j).wait_send()


def local(visibilities, counts, beam_inverse, kl_modes):
    tm = lax.axis_size("tm")
    nf = lax.axis_size("freq")
    _, stacks, band, window = visibilities.shape
    modes, _, _, sky_rows, _ = beam_inverse.shape
    kept = kl_modes.shape[1]
    share = stacks // tm
    lanes = share * band
    g, e = factors(modes * tm, 2 * window, tm // 2)
    any_space = pl.BlockSpec(memory_space=pl.ANY)
    rows_out = sky_rows // nf
    dma = pltpu.SemaphoreType.DMA
    filtered = pl.pallas_call(
        functools.partial(kernel, tm=tm, nf=nf, total=window * tm),
        out_shape=jax.ShapeDtypeStruct((modes, 2 * rows_out, kept), BF16),
        in_specs=[any_space] * 6,
        out_specs=pl.BlockSpec(memory_space=pltpu.VMEM),
        scratch_shapes=[
            pltpu.SMEM(counts.shape, jnp.int32),
            pltpu.VMEM((tm, 2, lanes, window), BF16),
            pltpu.VMEM(beam_inverse.shape, BF16),
            pltpu.VMEM(kl_modes.shape, BF16),
            pltpu.VMEM((modes, kept, nf * 128), BF16),
            pltpu.VMEM(g.shape[1:], BF16),
            pltpu.VMEM(e.shape, BF16),
            pltpu.VMEM((tm // 2, SUMS, lanes), F32),
            pltpu.VMEM((tm // 2, SUMS, lanes), F32),
            pltpu.VMEM((tm // 2, 2 * ROWS, lanes // 2), BF16),
            pltpu.VMEM((tm // 2, 2 * ROWS, lanes // 2), BF16),
            pltpu.VMEM((tm, 4 * modes, lanes // 2), BF16),
            pltpu.VMEM((tm, 4 * modes, lanes // 2), BF16),
            pltpu.VMEM((2 * modes * stacks, 128), F32),
            pltpu.VMEM((modes, 2 * stacks, 256), BF16),
            pltpu.VMEM((modes, nf, 2 * rows_out, 128), BF16),
            pltpu.VMEM((modes, nf, 2 * rows_out, 128), BF16),
            dma((tm,)), dma((modes,)), dma((4,)),
            dma((tm // 2,)), dma((tm // 2,)), pltpu.SemaphoreType.REGULAR, pltpu.SemaphoreType.REGULAR,
            dma((tm // 2,)), dma((tm // 2,)), dma((tm,)), dma((tm,)),
            dma((modes, nf)), dma((modes, nf)),
        ],
        compiler_params=pltpu.CompilerParams(
            collective_id=0, has_side_effects=True, vmem_limit_bytes=56 * 2**20),
    )(counts, visibilities.reshape(2, tm, lanes, window), beam_inverse, kl_modes, jnp.asarray(g), jnp.asarray(e))
    return filtered.reshape(modes, 2, rows_out, kept).transpose(2, 0, 1, 3)


def solution(mesh):
    in_specs = (
        P(None, None, "freq", "tm"),
        P(),
        P("tm", "freq", None, None, None),
        P("tm", None, None),
    )
    out_specs = P("freq", "tm", None, None)
    return jax.shard_map(local, mesh=mesh, in_specs=in_specs, out_specs=out_specs, check_vma=False)
```

```python
import functools
import math

import jax
import jax.numpy as jnp
import ml_dtypes
import numpy as np
from jax import lax
from jax.experimental import pallas as pl
from jax.experimental.pallas import tpu as pltpu
from jax.sharding import PartitionSpec as P

RANK = 17
STRONG = (7, 8, 9)
DATA = 2 * RANK
ROWS = DATA + 2 * len(STRONG)
SUMS = 40
TOGETHER = 2
AHEAD = 4
GREETED = 3
KNOWN = 1
F32 = jnp.float32
BF16 = jnp.bfloat16


def window_factors(modes, window, windows):
    total = window * windows
    step = 2.0 * math.pi / total
    m = np.arange(modes, dtype=np.float64)
    t = np.arange(window, dtype=np.float64)
    mc, tc = (modes - 1) / 2.0, (window - 1) / 2.0
    diag = -np.cos(math.pi * (2 * t + 1 - window) / total) * math.cos(math.pi * modes / total)
    off = np.sin(math.pi * (t[:-1] + 1) / total) * np.sin(math.pi * (window - 1 - t[:-1]) / total)
    _, vectors = np.linalg.eigh(np.diag(diag) + np.diag(off, 1) + np.diag(off, -1))
    return m, t, mc, tc, step, vectors


def prolate(modes, window, windows):
    m, t, mc, tc, step, vectors = window_factors(modes, window, windows)
    centred = np.exp(-1j * step * np.outer(m - mc, t - tc))
    strength = np.linalg.norm(centred @ vectors, axis=0)
    basis = vectors[:, np.argsort(-strength)[:RANK]].T
    basis = basis * np.sign(basis[:, :window // 3].sum(1))[:, None]
    expand = centred @ basis.T
    project = basis * np.exp(-1j * step * mc * (t - tc))[None]
    return m, tc, step, expand, project


def halves(x):
    x = np.round(x * 2.0**22) / 2.0**22
    high = x.astype(np.float32).astype(ml_dtypes.bfloat16)
    low = (x - high.astype(np.float64)).astype(np.float32).astype(ml_dtypes.bfloat16)
    return np.concatenate([high, low], 0)


def factors(modes, window, windows):
    m, tc, step, expand, project = prolate(modes, window, windows)
    weak = [(k, part) for part in (0, 1) for k in range(RANK) if k not in STRONG]
    strong = [(k, part) for part in (0, 1) for k in STRONG]
    lead = DATA - 32
    rows = weak[:lead] + strong + weak[lead:]
    g = np.zeros((SUMS, 2, window))
    for at, (k, part) in enumerate(rows):
        re, im = project[k].real, project[k].imag
        g[at] = (re, -im) if part == 0 else (im, re)
    e = np.zeros((modes, 2, windows, ROWS))
    for w in range(windows):
        turned = expand * np.exp(-1j * step * m * (w * window + tc))[:, None]
        for at, (k, part) in enumerate(rows):
            re, im = turned[:, k].real, turned[:, k].imag
            e[:, 0, w, at] = re if part == 0 else -im
            e[:, 1, w, at] = im if part == 0 else re
    e[..., DATA:] = e[..., lead:lead + 2 * len(STRONG)]
    g = g.reshape(SUMS, 2, 2, window // 2).transpose(2, 0, 1, 3)
    g = np.stack([halves(core.reshape(SUMS, window)) for core in g])
    return g, halves(e.reshape(2 * modes, windows * ROWS))


def kernel(
    countsh, vis, beam, kl, g, e, out,
    counts, visb, beamb, klb, klp, gb, eb, pairsend, pairrecv, ysend, yrecv, ssend, srecv, wf, wmat, skysend, skyrecv,
    vis_sem, beam_sem, misc_sem, ps_sem, pr_sem, x_sem, z_sem, ys_sem, yr_sem, ss_sem, sr_sem, ks_sem, kr_sem,
    *, tm, nf, total,
):
    me = lax.axis_index("tm")
    mf = lax.axis_index("freq")
    lanes = visb.shape[2]
    half = lanes // 2
    modes = beamb.shape[0]
    band = beamb.shape[1]
    window = visb.shape[3]

    core = me % 2
    chip = me // 2
    chips = tm // 2
    g_copy = pltpu.make_async_copy(g.at[core], gb, misc_sem.at[0])
    e_copy = pltpu.make_async_copy(e, eb, misc_sem.at[1])
    kl_copy = pltpu.make_async_copy(kl, klb, misc_sem.at[2])
    count_copy = pltpu.make_async_copy(countsh, counts, misc_sem.at[3])
    barrier = pltpu.get_barrier_semaphore()

    def at(dx, dy, dc):
        x, y = chip // 2, chip % 2
        return lax.rem(x + dx, chips // 2) * 4 + lax.rem(y + dy, 2) * 2 + lax.rem(core + dc, 2)

    steps = [(dx, dy) for dy in (1, 0) for dx in (2, 1, 3, 0) if (dx, dy) != (0, 0)]
    near = [(0, 1), (2, 0), (1, 0), (3, 0)]
    far = [(2, 1), (1, 1), (3, 1)]
    same = [at(dx, dy, 0) for dx, dy in far + near]
    chip_order = [j // 2 for j in same] + [chip]
    partner = at(0, 0, 1)
    others = [at(dx, dy, dc) for dx, dy in steps for dc in (1, 0)] + [partner]
    along_x = [at(dx, 0, 0) for dx in (2, 1, 3)]
    across = at(0, 1, 0)
    z, low_y = mf // 2, mf % 2
    along_z = [lax.rem(z + dz, nf // 2) * 2 + low_y for dz in (2, 1, 3)]
    beside = z * 2 + 1 - low_y
    bands = [lax.rem(z + dz, nf // 2) * 2 + lax.rem(low_y + dy, 2) for dy in (1, 0) for dz in (2, 1, 3)] + [beside]

    def signal(sem, **where):
        pl.semaphore_signal(sem, inc=1, device_id=where, device_id_type=pl.DeviceIdType.MESH)

    for j in along_x + [across, partner]:
        signal(barrier, tm=j)
    for j in along_z + [beside]:
        signal(barrier, freq=j)
    g_copy.start()

    def vis_copy(j):
        return pltpu.make_async_copy(vis.at[:, j], visb.at[j], vis_sem.at[j])

    def beam_copy(m):
        return pltpu.make_async_copy(beam.at[m], beamb.at[m], beam_sem.at[m])

    def chunk(k):
        return 2 * chip_order[k % chips] + (1 - core if k < chips else core)

    for k in range(AHEAD):
        vis_copy(chunk(k)).start()
    count_copy.start()

    def pair_copy(i):
        return pltpu.make_async_remote_copy(
            src_ref=pairsend.at[i], dst_ref=pairrecv.at[i], send_sem=ps_sem.at[i], recv_sem=pr_sem.at[i],
            device_id={"tm": partner}, device_id_type=pl.DeviceIdType.MESH)

    def y_copy(k):
        return pltpu.make_async_remote_copy(
            src_ref=ysend.at[k], dst_ref=yrecv.at[chip], send_sem=ys_sem.at[k], recv_sem=yr_sem.at[chip],
            device_id={"tm": same[k]}, device_id_type=pl.DeviceIdType.MESH)

    def y_from(s):
        return pltpu.make_async_remote_copy(
            src_ref=ysend.at[s // 2], dst_ref=yrecv.at[s // 2], send_sem=ys_sem.at[s // 2], recv_sem=yr_sem.at[s // 2],
            device_id={"tm": s}, device_id_type=pl.DeviceIdType.MESH)

    def s_copy(j):
        return pltpu.make_async_remote_copy(
            src_ref=ssend.at[j], dst_ref=srecv.at[me], send_sem=ss_sem.at[j], recv_sem=sr_sem.at[me],
            device_id={"tm": j}, device_id_type=pl.DeviceIdType.MESH)

    def s_from(s):
        return pltpu.make_async_remote_copy(
            src_ref=ssend.at[s], dst_ref=srecv.at[s], send_sem=ss_sem.at[s], recv_sem=sr_sem.at[s],
            device_id={"tm": s}, device_id_type=pl.DeviceIdType.MESH)

    def k_copy(m, j):
        return pltpu.make_async_remote_copy(
            src_ref=skysend.at[m, j], dst_ref=skyrecv.at[m, mf], send_sem=ks_sem.at[m, j], recv_sem=kr_sem.at[m, mf],
            device_id={"freq": j}, device_id_type=pl.DeviceIdType.MESH)

    def k_from(m, s):
        return pltpu.make_async_remote_copy(
            src_ref=skysend.at[m, s], dst_ref=skyrecv.at[m, s], send_sem=ks_sem.at[m, s], recv_sem=kr_sem.at[m, s],
            device_id={"freq": s}, device_id_type=pl.DeviceIdType.MESH)

    nt = (((1,), (1,)), ((), ()))

    def project(k):
        js = [chunk(i) for i in range(k, k + TOGETHER)]
        for j in js:
            vis_copy(j).wait()
        for i in range(k + AHEAD, min(k + AHEAD + TOGETHER, tm)):
            vis_copy(chunk(i)).start()
        y = 0.0
        for p in (0, 1):
            x = jnp.concatenate([visb[j, p] for j in js], 0)
            y = y + lax.dot_general(gb[:, p * window:(p + 1) * window], x, nt, preferred_element_type=F32)
        y = y[:SUMS] + y[SUMS:]
        return [y[:, i * lanes:(i + 1) * lanes] for i in range(TOGETHER)]

    g_copy.wait()
    for k in range(0, chips, TOGETHER):
        for i, y in enumerate(project(k)):
            pairsend[k + i] = y
        last = k + TOGETHER
        if k <= GREETED < last:
            pl.semaphore_wait(barrier, 9)
            for j in along_x:
                signal(x_sem, tm=j)
            for j in along_z:
                signal(z_sem, freq=j)
        if GREETED < last:
            for i in range(0 if k <= GREETED else k, last):
                pair_copy(i).start()
    row = lax.broadcasted_iota(jnp.int32, (ROWS - 32, lanes), 0) + 32

    def merge(k, own):
        y = own + pairrecv[k]
        low = y[:ROWS - 32]
        low = low - low.astype(BF16).astype(F32)
        y = jnp.concatenate([y[:32], jnp.where(row < DATA, y[32:], low)], 0)
        y = jnp.concatenate([y[:, :half], y[:, half:]], 0).astype(BF16)
        if k < chips - 1:
            ysend[k] = y
        else:
            yrecv[chip] = y

    sent = 0
    for k in range(0, chips, TOGETHER):
        own = project(k + chips)
        for i in range(TOGETHER):
            pair_copy(k + i).wait_recv()
        for i in range(TOGETHER):
            merge(k + i, own[i])
        if k + TOGETHER > KNOWN:
            if not sent:
                pl.semaphore_wait(x_sem, 3)
            for i in range(sent, min(k + TOGETHER, chips - 1)):
                y_copy(i).start()
            sent = k + TOGETHER
    e_copy.start()
    kl_copy.start()
    for m in range(modes):
        beam_copy(m).start()

    kl_copy.wait()

    def spread(m, c):
        zero = jnp.zeros((klb.shape[1], 128 - band), BF16)
        for s in range(nf):
            klp[m, :, s * 128:(s + 1) * 128] = jnp.concatenate([klb[m, :, s * band:(s + 1) * band], zero], 1)
        return c

    lax.fori_loop(0, modes, spread, 0)

    lane = lax.broadcasted_iota(jnp.int32, (1, lanes), 1) // band
    share = lanes // band
    count_copy.wait()
    count = jnp.zeros((1, lanes), F32)
    for i in range(share):
        count = jnp.where(lane == i, counts[me * share + i].astype(F32), count)
    factor = jnp.sqrt(count) * (1.0 / math.sqrt(128.0 * total))

    e_copy.wait()
    for j in same:
        y_from(j).wait_recv()
    parts = []
    for h in range(2):
        y = yrecv[:, h * ROWS:(h + 1) * ROWS].reshape(chips * ROWS, half)
        x = jnp.dot(eb[...], y, preferred_element_type=F32)
        n = x.shape[0] // 2
        parts.append((x[:n] + x[n:]) * factor[:, h * half:(h + 1) * half])
    mq = 2 * modes
    for j in range(tm):
        ssend[j] = jnp.concatenate([p[j * mq:(j + 1) * mq] for p in parts], 0).astype(BF16)

    for j in others:
        s_copy(j).start()
    srecv[me] = ssend[me]

    for j in others:
        s_from(j).wait_recv()

    stacks = tm * share
    quarter = share // 2

    zero = jnp.zeros((2 * mq, 128 - band), F32)
    def unpack(i, c):
        for s in range(4):
            s = 4 * i + s
            x = srecv[s].astype(F32)
            for b in range(quarter):
                piece = jnp.concatenate([x[:, b * band:(b + 1) * band], zero], 1)
                for h in range(2):
                    wf[pl.ds(s * share + h * quarter + b, mq, stride=stacks), :] = piece[h * mq:(h + 1) * mq]
        return c

    lax.fori_loop(0, tm // 4, unpack, 0)
    for m in range(modes):
        s0 = wf[2 * m * stacks:(2 * m + 1) * stacks]
        s1 = wf[(2 * m + 1) * stacks:(2 * m + 2) * stacks]
        wmat[m, :stacks] = jnp.concatenate([s0, s1], 1).astype(BF16)
        wmat[m, stacks:] = jnp.concatenate([-s1, s0], 1).astype(BF16)

    pl.semaphore_wait(z_sem, 3)

    sky_rows = beamb.shape[3]
    column = lax.broadcasted_iota(jnp.int32, (sky_rows, 256), 1) % 128
    rows_out = sky_rows // nf

    def one_mode(m, c):
        beam_copy(m).wait()
        x = beamb[m]
        x = jnp.concatenate([x[:, 0], x[:, 1]], 2).reshape(band * sky_rows, 2 * stacks)
        z = jnp.dot(x, wmat[m], preferred_element_type=F32)
        acc = jnp.zeros((sky_rows, 256), F32)
        for f in range(band):
            acc = jnp.where(column == f, z[f * sky_rows:(f + 1) * sky_rows], acc)
        for j in range(nf):
            rows = acc[j * rows_out:(j + 1) * rows_out]
            skysend[m, j] = jnp.concatenate([rows[:, :128], rows[:, 128:]], 0).astype(BF16)

        for j in bands:
            k_copy(m, j).start()
        skyrecv[m, mf] = skysend[m, mf]
        return c

    lax.fori_loop(0, modes, one_mode, 0)

    for m in range(modes):
        for j in bands:
            k_from(m, j).wait_recv()
        rows = jnp.concatenate([skyrecv[m, s] for s in range(nf)], 1)
        out[m] = lax.dot_general(rows, klp[m], nt, preferred_element_type=F32).astype(BF16)

    lax.fori_loop(0, chips, lambda i, c: (pair_copy(i).wait_send(), c)[1], 0)
    for k in range(chips - 1):
        y_copy(k).wait_send()
    for j in others:
        s_copy(j).wait_send()
    for j in bands:
        for m in range(modes):
            k_copy(m, j).wait_send()


def local(visibilities, counts, beam_inverse, kl_modes):
    tm = lax.axis_size("tm")
    nf = lax.axis_size("freq")
    _, stacks, band, window = visibilities.shape
    modes, _, _, sky_rows, _ = beam_inverse.shape
    kept = kl_modes.shape[1]
    share = stacks // tm
    lanes = share * band
    g, e = factors(modes * tm, 2 * window, tm // 2)
    any_space = pl.BlockSpec(memory_space=pl.ANY)
    rows_out = sky_rows // nf
    dma = pltpu.SemaphoreType.DMA
    filtered = pl.pallas_call(
        functools.partial(kernel, tm=tm, nf=nf, total=window * tm),
        out_shape=jax.ShapeDtypeStruct((modes, 2 * rows_out, kept), BF16),
        in_specs=[any_space] * 6,
        out_specs=pl.BlockSpec(memory_space=pltpu.VMEM),
        scratch_shapes=[
            pltpu.SMEM(counts.shape, jnp.int32),
            pltpu.VMEM((tm, 2, lanes, window), BF16),
            pltpu.VMEM(beam_inverse.shape, BF16),
            pltpu.VMEM(kl_modes.shape, BF16),
            pltpu.VMEM((modes, kept, nf * 128), BF16),
            pltpu.VMEM(g.shape[1:], BF16),
            pltpu.VMEM(e.shape, BF16),
            pltpu.VMEM((tm // 2, SUMS, lanes), F32),
            pltpu.VMEM((tm // 2, SUMS, lanes), F32),
            pltpu.VMEM((tm // 2, 2 * ROWS, lanes // 2), BF16),
            pltpu.VMEM((tm // 2, 2 * ROWS, lanes // 2), BF16),
            pltpu.VMEM((tm, 4 * modes, lanes // 2), BF16),
            pltpu.VMEM((tm, 4 * modes, lanes // 2), BF16),
            pltpu.VMEM((2 * modes * stacks, 128), F32),
            pltpu.VMEM((modes, 2 * stacks, 256), BF16),
            pltpu.VMEM((modes, nf, 2 * rows_out, 128), BF16),
            pltpu.VMEM((modes, nf, 2 * rows_out, 128), BF16),
            dma((tm,)), dma((modes,)), dma((4,)),
            dma((tm // 2,)), dma((tm // 2,)), pltpu.SemaphoreType.REGULAR, pltpu.SemaphoreType.REGULAR,
            dma((tm // 2,)), dma((tm // 2,)), dma((tm,)), dma((tm,)),
            dma((modes, nf)), dma((modes, nf)),
        ],
        compiler_params=pltpu.CompilerParams(
            collective_id=0, has_side_effects=True, vmem_limit_bytes=56 * 2**20),
    )(counts, visibilities.reshape(2, tm, lanes, window), beam_inverse, kl_modes, jnp.asarray(g), jnp.asarray(e))
    return filtered.reshape(modes, 2, rows_out, kept).transpose(2, 0, 1, 3)


def solution(mesh):
    in_specs = (
        P(None, None, "freq", "tm"),
        P(),
        P("tm", "freq", None, None, None),
        P("tm", None, None),
    )
    out_specs = P("freq", "tm", None, None)
    return jax.shard_map(local, mesh=mesh, in_specs=in_specs, out_specs=out_specs, check_vma=False)
```

```python
import functools
import math

import jax
import jax.numpy as jnp
import ml_dtypes
import numpy as np
from jax import lax
from jax.experimental import pallas as pl
from jax.experimental.pallas import tpu as pltpu
from jax.sharding import PartitionSpec as P

RANK = 17
STRONG = (7, 8, 9)
DATA = 2 * RANK
ROWS = DATA + 2 * len(STRONG)
SUMS = 40
TOGETHER = 2
AHEAD = 6
GREETED = 3
KNOWN = 1
F32 = jnp.float32
BF16 = jnp.bfloat16


def window_factors(modes, window, windows):
    total = window * windows
    step = 2.0 * math.pi / total
    m = np.arange(modes, dtype=np.float64)
    t = np.arange(window, dtype=np.float64)
    mc, tc = (modes - 1) / 2.0, (window - 1) / 2.0
    diag = -np.cos(math.pi * (2 * t + 1 - window) / total) * math.cos(math.pi * modes / total)
    off = np.sin(math.pi * (t[:-1] + 1) / total) * np.sin(math.pi * (window - 1 - t[:-1]) / total)
    _, vectors = np.linalg.eigh(np.diag(diag) + np.diag(off, 1) + np.diag(off, -1))
    return m, t, mc, tc, step, vectors


def prolate(modes, window, windows):
    m, t, mc, tc, step, vectors = window_factors(modes, window, windows)
    centred = np.exp(-1j * step * np.outer(m - mc, t - tc))
    strength = np.linalg.norm(centred @ vectors, axis=0)
    basis = vectors[:, np.argsort(-strength)[:RANK]].T
    basis = basis * np.sign(basis[:, :window // 3].sum(1))[:, None]
    expand = centred @ basis.T
    project = basis * np.exp(-1j * step * mc * (t - tc))[None]
    return m, tc, step, expand, project


def halves(x):
    x = np.round(x * 2.0**22) / 2.0**22
    high = x.astype(np.float32).astype(ml_dtypes.bfloat16)
    low = (x - high.astype(np.float64)).astype(np.float32).astype(ml_dtypes.bfloat16)
    return np.concatenate([high, low], 0)


def factors(modes, window, windows):
    m, tc, step, expand, project = prolate(modes, window, windows)
    weak = [(k, part) for part in (0, 1) for k in range(RANK) if k not in STRONG]
    strong = [(k, part) for part in (0, 1) for k in STRONG]
    lead = DATA - 32
    rows = weak[:lead] + strong + weak[lead:]
    g = np.zeros((SUMS, 2, window))
    for at, (k, part) in enumerate(rows):
        re, im = project[k].real, project[k].imag
        g[at] = (re, -im) if part == 0 else (im, re)
    e = np.zeros((modes, 2, windows, ROWS))
    for w in range(windows):
        turned = expand * np.exp(-1j * step * m * (w * window + tc))[:, None]
        for at, (k, part) in enumerate(rows):
            re, im = turned[:, k].real, turned[:, k].imag
            e[:, 0, w, at] = re if part == 0 else -im
            e[:, 1, w, at] = im if part == 0 else re
    e[..., DATA:] = e[..., lead:lead + 2 * len(STRONG)]
    g = g.reshape(SUMS, 2, 2, window // 2).transpose(2, 0, 1, 3)
    g = np.stack([halves(core.reshape(SUMS, window)) for core in g])
    return g, halves(e.reshape(2 * modes, windows * ROWS))


def kernel(
    countsh, vis, beam, kl, g, e, out,
    counts, visb, beamb, klb, klp, gb, eb, pairsend, pairrecv, ysend, yrecv, ssend, srecv, wf, wmat, skysend, skyrecv,
    vis_sem, beam_sem, misc_sem, ps_sem, pr_sem, x_sem, z_sem, ys_sem, yr_sem, ss_sem, sr_sem, ks_sem, kr_sem,
    *, tm, nf, total,
):
    me = lax.axis_index("tm")
    mf = lax.axis_index("freq")
    lanes = visb.shape[2]
    half = lanes // 2
    modes = beamb.shape[0]
    band = beamb.shape[1]
    window = visb.shape[3]

    core = me % 2
    chip = me // 2
    chips = tm // 2
    g_copy = pltpu.make_async_copy(g.at[core], gb, misc_sem.at[0])
    e_copy = pltpu.make_async_copy(e, eb, misc_sem.at[1])
    kl_copy = pltpu.make_async_copy(kl, klb, misc_sem.at[2])
    count_copy = pltpu.make_async_copy(countsh, counts, misc_sem.at[3])
    barrier = pltpu.get_barrier_semaphore()

    def at(dx, dy, dc):
        x, y = chip // 2, chip % 2
        return lax.rem(x + dx, chips // 2) * 4 + lax.rem(y + dy, 2) * 2 + lax.rem(core + dc, 2)

    steps = [(dx, dy) for dy in (1, 0) for dx in (2, 1, 3, 0) if (dx, dy) != (0, 0)]
    near = [(0, 1), (2, 0), (1, 0), (3, 0)]
    far = [(2, 1), (1, 1), (3, 1)]
    same = [at(dx, dy, 0) for dx, dy in far + near]
    chip_order = [j // 2 for j in same] + [chip]
    partner = at(0, 0, 1)
    others = [at(dx, dy, dc) for dx, dy in steps for dc in (1, 0)] + [partner]
    along_x = [at(dx, 0, 0) for dx in (2, 1, 3)]
    across = at(0, 1, 0)
    z, low_y = mf // 2, mf % 2
    along_z = [lax.rem(z + dz, nf // 2) * 2 + low_y for dz in (2, 1, 3)]
    beside = z * 2 + 1 - low_y
    bands = [lax.rem(z + dz, nf // 2) * 2 + lax.rem(low_y + dy, 2) for dy in (1, 0) for dz in (2, 1, 3)] + [beside]

    def signal(sem, **where):
        pl.semaphore_signal(sem, inc=1, device_id=where, device_id_type=pl.DeviceIdType.MESH)

    for j in along_x + [across, partner]:
        signal(barrier, tm=j)
    for j in along_z + [beside]:
        signal(barrier, freq=j)
    g_copy.start()

    def vis_copy(j):
        return pltpu.make_async_copy(vis.at[:, j], visb.at[j], vis_sem.at[j])

    def beam_copy(m):
        return pltpu.make_async_copy(beam.at[m], beamb.at[m], beam_sem.at[m])

    def chunk(k):
        return 2 * chip_order[k % chips] + (1 - core if k < chips else core)

    for k in range(AHEAD):
        vis_copy(chunk(k)).start()
    count_copy.start()

    def pair_copy(i):
        return pltpu.make_async_remote_copy(
            src_ref=pairsend.at[i], dst_ref=pairrecv.at[i], send_sem=ps_sem.at[i], recv_sem=pr_sem.at[i],
            device_id={"tm": partner}, device_id_type=pl.DeviceIdType.MESH)

    def y_copy(k):
        return pltpu.make_async_remote_copy(
            src_ref=ysend.at[k], dst_ref=yrecv.at[chip], send_sem=ys_sem.at[k], recv_sem=yr_sem.at[chip],
            device_id={"tm": same[k]}, device_id_type=pl.DeviceIdType.MESH)

    def y_from(s):
        return pltpu.make_async_remote_copy(
            src_ref=ysend.at[s // 2], dst_ref=yrecv.at[s // 2], send_sem=ys_sem.at[s // 2], recv_sem=yr_sem.at[s // 2],
            device_id={"tm": s}, device_id_type=pl.DeviceIdType.MESH)

    def s_copy(j):
        return pltpu.make_async_remote_copy(
            src_ref=ssend.at[j], dst_ref=srecv.at[me], send_sem=ss_sem.at[j], recv_sem=sr_sem.at[me],
            device_id={"tm": j}, device_id_type=pl.DeviceIdType.MESH)

    def s_from(s):
        return pltpu.make_async_remote_copy(
            src_ref=ssend.at[s], dst_ref=srecv.at[s], send_sem=ss_sem.at[s], recv_sem=sr_sem.at[s],
            device_id={"tm": s}, device_id_type=pl.DeviceIdType.MESH)

    def k_copy(m, j):
        return pltpu.make_async_remote_copy(
            src_ref=skysend.at[m, j], dst_ref=skyrecv.at[m, mf], send_sem=ks_sem.at[m, j], recv_sem=kr_sem.at[m, mf],
            device_id={"freq": j}, device_id_type=pl.DeviceIdType.MESH)

    def k_from(m, s):
        return pltpu.make_async_remote_copy(
            src_ref=skysend.at[m, s], dst_ref=skyrecv.at[m, s], send_sem=ks_sem.at[m, s], recv_sem=kr_sem.at[m, s],
            device_id={"freq": s}, device_id_type=pl.DeviceIdType.MESH)

    nt = (((1,), (1,)), ((), ()))

    def project(k):
        js = [chunk(i) for i in range(k, k + TOGETHER)]
        for j in js:
            vis_copy(j).wait()
        for i in range(k + AHEAD, min(k + AHEAD + TOGETHER, tm)):
            vis_copy(chunk(i)).start()
        y = 0.0
        for p in (0, 1):
            x = jnp.concatenate([visb[j, p] for j in js], 0)
            y = y + lax.dot_general(gb[:, p * window:(p + 1) * window], x, nt, preferred_element_type=F32)
        y = y[:SUMS] + y[SUMS:]
        return [y[:, i * lanes:(i + 1) * lanes] for i in range(TOGETHER)]

    g_copy.wait()
    for k in range(0, chips, TOGETHER):
        for i, y in enumerate(project(k)):
            pairsend[k + i] = y
        last = k + TOGETHER
        if k <= GREETED < last:
            pl.semaphore_wait(barrier, 9)
            for j in along_x:
                signal(x_sem, tm=j)
            for j in along_z:
                signal(z_sem, freq=j)
        if GREETED < last:
            for i in range(0 if k <= GREETED else k, last):
                pair_copy(i).start()
    row = lax.broadcasted_iota(jnp.int32, (ROWS - 32, lanes), 0) + 32

    def merge(k, own):
        y = own + pairrecv[k]
        low = y[:ROWS - 32]
        low = low - low.astype(BF16).astype(F32)
        y = jnp.concatenate([y[:32], jnp.where(row < DATA, y[32:], low)], 0)
        y = jnp.concatenate([y[:, :half], y[:, half:]], 0).astype(BF16)
        if k < chips - 1:
            ysend[k] = y
        else:
            yrecv[chip] = y

    sent = 0
    for k in range(0, chips, TOGETHER):
        own = project(k + chips)
        for i in range(TOGETHER):
            pair_copy(k + i).wait_recv()
        for i in range(TOGETHER):
            merge(k + i, own[i])
        if k + TOGETHER > KNOWN:
            if not sent:
                pl.semaphore_wait(x_sem, 3)
            for i in range(sent, min(k + TOGETHER, chips - 1)):
                y_copy(i).start()
            sent = k + TOGETHER
    e_copy.start()
    kl_copy.start()
    for m in range(modes):
        beam_copy(m).start()

    kl_copy.wait()

    def spread(m, c):
        zero = jnp.zeros((klb.shape[1], 128 - band), BF16)
        for s in range(nf):
            klp[m, :, s * 128:(s + 1) * 128] = jnp.concatenate([klb[m, :, s * band:(s + 1) * band], zero], 1)
        return c

    lax.fori_loop(0, modes, spread, 0)

    lane = lax.broadcasted_iota(jnp.int32, (1, lanes), 1) // band
    share = lanes // band
    count_copy.wait()
    count = jnp.zeros((1, lanes), F32)
    for i in range(share):
        count = jnp.where(lane == i, counts[me * share + i].astype(F32), count)
    factor = jnp.sqrt(count) * (1.0 / math.sqrt(128.0 * total))

    e_copy.wait()
    for j in same:
        y_from(j).wait_recv()
    parts = []
    for h in range(2):
        y = yrecv[:, h * ROWS:(h + 1) * ROWS].reshape(chips * ROWS, half)
        x = jnp.dot(eb[...], y, preferred_element_type=F32)
        n = x.shape[0] // 2
        parts.append((x[:n] + x[n:]) * factor[:, h * half:(h + 1) * half])
    mq = 2 * modes
    for j in range(tm):
        ssend[j] = jnp.concatenate([p[j * mq:(j + 1) * mq] for p in parts], 0).astype(BF16)

    for j in others:
        s_copy(j).start()
    srecv[me] = ssend[me]

    for j in others:
        s_from(j).wait_recv()

    stacks = tm * share
    quarter = share // 2

    zero = jnp.zeros((2 * mq, 128 - band), F32)
    def unpack(i, c):
        for s in range(4):
            s = 4 * i + s
            x = srecv[s].astype(F32)
            for b in range(quarter):
                piece = jnp.concatenate([x[:, b * band:(b + 1) * band], zero], 1)
                for h in range(2):
                    wf[pl.ds(s * share + h * quarter + b, mq, stride=stacks), :] = piece[h * mq:(h + 1) * mq]
        return c

    lax.fori_loop(0, tm // 4, unpack, 0)
    for m in range(modes):
        s0 = wf[2 * m * stacks:(2 * m + 1) * stacks]
        s1 = wf[(2 * m + 1) * stacks:(2 * m + 2) * stacks]
        wmat[m, :stacks] = jnp.concatenate([s0, s1], 1).astype(BF16)
        wmat[m, stacks:] = jnp.concatenate([-s1, s0], 1).astype(BF16)

    pl.semaphore_wait(z_sem, 3)

    sky_rows = beamb.shape[3]
    column = lax.broadcasted_iota(jnp.int32, (sky_rows, 256), 1) % 128
    rows_out = sky_rows // nf

    def one_mode(m, c):
        beam_copy(m).wait()
        x = beamb[m]
        x = jnp.concatenate([x[:, 0], x[:, 1]], 2).reshape(band * sky_rows, 2 * stacks)
        z = jnp.dot(x, wmat[m], preferred_element_type=F32)
        acc = jnp.zeros((sky_rows, 256), F32)
        for f in range(band):
            acc = jnp.where(column == f, z[f * sky_rows:(f + 1) * sky_rows], acc)
        for j in range(nf):
            rows = acc[j * rows_out:(j + 1) * rows_out]
            skysend[m, j] = jnp.concatenate([rows[:, :128], rows[:, 128:]], 0).astype(BF16)

        for j in bands:
            k_copy(m, j).start()
        skyrecv[m, mf] = skysend[m, mf]
        return c

    lax.fori_loop(0, modes, one_mode, 0)

    lax.fori_loop(0, chips, lambda i, c: (pair_copy(i).wait_send(), c)[1], 0)
    for k in range(chips - 1):
        y_copy(k).wait_send()
    for j in others:
        s_copy(j).wait_send()

    for m in range(modes):
        for j in bands:
            k_from(m, j).wait_recv()
        rows = jnp.concatenate([skyrecv[m, s] for s in range(nf)], 1)
        out[m] = lax.dot_general(rows, klp[m], nt, preferred_element_type=F32).astype(BF16)

    for j in bands:
        for m in range(modes):
            k_copy(m, j).wait_send()


def local(visibilities, counts, beam_inverse, kl_modes):
    tm = lax.axis_size("tm")
    nf = lax.axis_size("freq")
    _, stacks, band, window = visibilities.shape
    modes, _, _, sky_rows, _ = beam_inverse.shape
    kept = kl_modes.shape[1]
    share = stacks // tm
    lanes = share * band
    g, e = factors(modes * tm, 2 * window, tm // 2)
    any_space = pl.BlockSpec(memory_space=pl.ANY)
    rows_out = sky_rows // nf
    dma = pltpu.SemaphoreType.DMA
    filtered = pl.pallas_call(
        functools.partial(kernel, tm=tm, nf=nf, total=window * tm),
        out_shape=jax.ShapeDtypeStruct((modes, 2 * rows_out, kept), BF16),
        in_specs=[any_space] * 6,
        out_specs=pl.BlockSpec(memory_space=pltpu.VMEM),
        scratch_shapes=[
            pltpu.SMEM(counts.shape, jnp.int32),
            pltpu.VMEM((tm, 2, lanes, window), BF16),
            pltpu.VMEM(beam_inverse.shape, BF16),
            pltpu.VMEM(kl_modes.shape, BF16),
            pltpu.VMEM((modes, kept, nf * 128), BF16),
            pltpu.VMEM(g.shape[1:], BF16),
            pltpu.VMEM(e.shape, BF16),
            pltpu.VMEM((tm // 2, SUMS, lanes), F32),
            pltpu.VMEM((tm // 2, SUMS, lanes), F32),
            pltpu.VMEM((tm // 2, 2 * ROWS, lanes // 2), BF16),
            pltpu.VMEM((tm // 2, 2 * ROWS, lanes // 2), BF16),
            pltpu.VMEM((tm, 4 * modes, lanes // 2), BF16),
            pltpu.VMEM((tm, 4 * modes, lanes // 2), BF16),
            pltpu.VMEM((2 * modes * stacks, 128), F32),
            pltpu.VMEM((modes, 2 * stacks, 256), BF16),
            pltpu.VMEM((modes, nf, 2 * rows_out, 128), BF16),
            pltpu.VMEM((modes, nf, 2 * rows_out, 128), BF16),
            dma((tm,)), dma((modes,)), dma((4,)),
            dma((tm // 2,)), dma((tm // 2,)), pltpu.SemaphoreType.REGULAR, pltpu.SemaphoreType.REGULAR,
            dma((tm // 2,)), dma((tm // 2,)), dma((tm,)), dma((tm,)),
            dma((modes, nf)), dma((modes, nf)),
        ],
        compiler_params=pltpu.CompilerParams(
            collective_id=0, has_side_effects=True, vmem_limit_bytes=56 * 2**20),
    )(counts, visibilities.reshape(2, tm, lanes, window), beam_inverse, kl_modes, jnp.asarray(g), jnp.asarray(e))
    return filtered.reshape(modes, 2, rows_out, kept).transpose(2, 0, 1, 3)


def solution(mesh):
    in_specs = (
        P(None, None, "freq", "tm"),
        P(),
        P("tm", "freq", None, None, None),
        P("tm", None, None),
    )
    out_specs = P("freq", "tm", None, None)
    return jax.shard_map(local, mesh=mesh, in_specs=in_specs, out_specs=out_specs, check_vma=False)
```
